256 devices in a mesh: grp: 8 (over z), seq: 32 (over x, y, core).
Axes of the slice: x: 4, y: 4, z: 8, core: 2. Of those that a mesh axis runs over, the one named last changes fastest.
Arguments:
- frames: bfloat16 [8, 16384, 1024], P('grp', 'seq'), may hold values from -6 to 6
- begins: int32 [8, 16384], P('grp', 'seq'), may hold values from 0 to 1, as said below
- owner: int32 [8, 2048, 1], P('grp', 'seq'), may hold values from 0 to 31; in each aligned block of 64 rows (0 to 63, 64 to 127, ..., all dimensions but the last counted through in order) at most 4 rows name the same one
- conv_kernel: float32 [9, 1024], replicated, may hold values from -2 to 2
- norm_gain: float32 [1024], replicated, may hold values from 0.25 to 1.75
- w_qkv: bfloat16 [1024, 3072], replicated, may hold values from -0.1875 to 0.1875
- w_out: bfloat16 [1024, 1024], replicated, may hold values from -1 to 1
- cotangent: bfloat16 [8, 4096, 1024], P('grp', 'seq'), may hold values from -6 to 6
Outputs:
- audio_rows: bfloat16 [8, 4096, 1024], P('grp', 'seq')
- out_grad: bfloat16 [1024, 1024], replicated
The draws below stay inside these ranges and needn't reach their ends.
Inputs may be any that keep to these rules, and one draw needn't show every extreme that they name: `begins`: the first frame of every group is 1; utterances run 16 frames or more and fewer than 1536, the last one cut by the group's end. At most 4 pooled rows of one device go to one owner.
All inputs are finite; a program needn't handle non-finite values.
Results may differ from the reference program's by a relative error of at most 0.017.
The reference program's roundings to bfloat16 on the way (of `hidden`, `normed`, `qkv`, `weights`, `attn`, `pooled` and `row_grads`) count: a program that leaves them out, or rounds other values in their place, can miss the bound.
Values may be sent and summed in bfloat16 or wider, within the bound.
A program may use at most 128 MiB of HBM per device.

```python
import math
import jax
import jax.numpy as jnp
import numpy as np
from jax import lax

D = 1024
HEADS = 8
KERNEL = 9
HEAD_DIM = 128
BLOCK_LEN = 32
LEFT_BLOCKS = 2
SUB = 8
FDEV = 512
ROWS_DEV = 64
CAP = 4
OWN_SLOTS = 128
GROUP_FR = 16384
GROUP_ROWS = 2048
N_GRP = 8
N_SEQ = 32


def draw_begins(key, part):
    key = jax.random.fold_in(key, 11)
    length_key, flag_key, place_key = jax.random.split(key, 3)
    length_count = GROUP_FR // 16 + 1
    lengths = jax.random.randint(length_key, (N_GRP, length_count), 16, 2 * FDEV + 1, dtype=jnp.int32)
    row_starts = jnp.cumsum(lengths, axis=1) - lengths
    row_starts = jnp.minimum(row_starts, GROUP_FR)

    def mark_starts(positions):
        return jnp.zeros((GROUP_FR + 1,), jnp.int32).at[positions].set(1)[:GROUP_FR]
    marks = jax.vmap(mark_starts)(row_starts)
    device_ids = jnp.arange(N_SEQ + 1, dtype=jnp.int32)
    flags = jax.random.randint(flag_key, (N_GRP, N_SEQ + 1), 0, 4, dtype=jnp.int32) > 0
    flags = flags & (device_ids[None, :] >= 1) & (device_ids[None, :] < N_SEQ)
    places = jax.random.randint(place_key, (N_GRP, N_SEQ + 1), 1, 5, dtype=jnp.int32)
    position = jnp.arange(GROUP_FR, dtype=jnp.int32)
    nearest = (position + 16) // FDEV
    boundary = nearest * FDEV
    window = position < boundary + 20
    near_flag = jnp.take_along_axis(flags, jnp.broadcast_to(nearest[None, :], (N_GRP, GROUP_FR)), axis=1)
    near_place = jnp.take_along_axis(places, jnp.broadcast_to(nearest[None, :], (N_GRP, GROUP_FR)), axis=1)
    cleared = near_flag & window[None, :]
    forced = (position[None, :] == boundary[None, :] + near_place).astype(jnp.int32)
    return jnp.where(cleared, forced, marks).astype(jnp.int32)


def draw_w_qkv(key, part):
    key = jax.random.fold_in(key, 23)
    base_key = jax.random.fold_in(key, 0)
    root_width = jnp.sqrt(jnp.float32(D))
    values = jax.random.truncated_normal(base_key, -6.0, 6.0, (D, 3 * D), jnp.float32) / root_width
    return values.astype(jnp.bfloat16)


def block_levels(rng, dims, pieces, smallest, largest):
    level, own = 1.0, jax.random.fold_in(rng, 6)
    for dim, parts in pieces:
        steps = jnp.exp(jax.random.uniform(jax.random.fold_in(own, dim), (parts,), jnp.float32, smallest / len(pieces), largest / len(pieces)))
        level = level * jnp.repeat(steps, dims[dim] // parts).reshape([-1 if axis == dim else 1 for axis in range(len(dims))])
    return level


def assign_block(stream_key, own, number, rows, count, top, bound, skew):
    sequence = jax.random.permutation(stream_key, count)
    heavy_load, usual = shares(count, rows * top, bound, skew, True), shares(count, rows * top, bound, skew, False)
    places = jnp.arange(count)

    def named(tallies, turn):
        used = int((tallies > 0).sum())
        fixed = max(1, used // 4)
        moved = fixed + (places - fixed + turn * (used - fixed)) % max(1, count - fixed)
        return jnp.zeros((count,), jnp.int32).at[sequence[jnp.where(places < fixed, places, moved)]].set(jnp.asarray(tallies, jnp.int32))

    tallies = jnp.where(number % 4 == 0, named(heavy_load, number // 4), named(usual, number - number // 4 - 1))
    mixed = jax.random.permutation(jax.random.fold_in(own, 3), count)
    donor, receiver = mixed[0:count // 2 * 2:2], mixed[1:count // 2 * 2:2]
    margin = jnp.minimum(tallies[donor] - 1, bound - tallies[receiver]) // 2
    margin = jnp.where((donor == sequence[0]) | (receiver == sequence[0]) | (tallies[receiver] == 0), 0, jnp.maximum(margin, 0))
    moved = jax.random.randint(jax.random.fold_in(own, 4), (count // 2,), 0, 1 << 20) % (margin + 1)
    tallies = tallies.at[donor].add(-moved).at[receiver].add(moved)
    members = jnp.searchsorted(jnp.cumsum(tallies), jnp.arange(rows * top), side="right").astype(jnp.int32)
    grid = members.reshape(top, rows).T
    grid = grid[jax.random.permutation(jax.random.fold_in(own, 1), rows)]
    turn = jax.random.randint(jax.random.fold_in(own, 2), (rows, 1), 0, top)
    return jnp.take_along_axis(grid, (jnp.arange(top)[None, :] + turn) % top, axis=1)


def shares(number_of, total, limit, skew, full):
    weights = [(1 << 20) // math.isqrt(standing ** skew) + 1 for standing in range(1, number_of + 1)]
    largest = limit if full else min(limit, max(-(-total // number_of), total * weights[0] // sum(weights)))
    least = 1 if total - largest >= number_of - 1 else 0
    counts, rest = [largest] + [least] * (number_of - 1), total - largest - least * (number_of - 1)
    while rest > 0:
        free = [i for i in range(1, number_of) if counts[i] < largest] or [i for i in range(1, number_of) if counts[i] < limit]
        mass, budget = sum([weights[i] for i in free]), rest
        for i in free:
            more = min(limit - counts[i], max(1, budget * weights[i] // mass), rest)
            counts[i] = counts[i] + more
            rest = rest - more
    return np.array(counts)


def scatter_about(own_key, shape, scale, bound, cuts=(), held_as=jnp.bfloat16):
    entries = scale * jax.random.normal(own_key, shape, jnp.float32)
    if cuts:
        entries = entries * block_levels(own_key, shape, cuts, -0.22, 0.18)
    return jnp.clip(entries, -bound, bound).astype(held_as)


def setup_inputs(seed: int = 0) -> dict:
    splits = jax.random.split(jax.random.key(seed), 9)
    frames = scatter_about(splits[0], (N_GRP, GROUP_FR, D), 1.0, 6.0, ((0, 8), (1, 32)))
    begins = draw_begins(jax.random.fold_in(splits[8], 71), 0)
    owner_keys = jax.random.split(jax.random.fold_in(splits[2], 1), N_GRP * GROUP_ROWS // ROWS_DEV)
    owner_turns = jax.random.permutation(jax.random.fold_in(splits[2], 3), N_GRP * GROUP_ROWS // ROWS_DEV)
    owner = jax.vmap(lambda own, number: assign_block(jax.random.fold_in(splits[2], 2), own, number, ROWS_DEV, N_SEQ, 1, CAP, 2))(owner_keys, owner_turns).reshape((N_GRP, GROUP_ROWS, 1))
    conv_kernel = scatter_about(splits[3], (KERNEL, D), KERNEL ** -0.5, 2.0, (), jnp.float32)
    norm_gain = jnp.clip(1.0 + 0.15 * jax.random.normal(splits[4], (D,), jnp.float32), 0.25, 1.75)
    w_qkv = draw_w_qkv(jax.random.fold_in(splits[8], 71), 0)
    w_out = scatter_about(splits[6], (D, D), (D / 36) ** -0.5, 1.0)
    cotangent = scatter_about(splits[7], (N_GRP, N_SEQ * OWN_SLOTS, D), 1.0, 6.0, ((0, 8), (1, 32)))
    return {"frames": frames, "begins": begins, "owner": owner, "conv_kernel": conv_kernel, "norm_gain": norm_gain, "w_qkv": w_qkv, "w_out": w_out, "cotangent": cotangent}


def utterance_bounds(begins):
    frame_idx = jnp.arange(GROUP_FR, dtype=jnp.int32)[None, :]
    begin_mask = begins == 1
    start_idx = lax.cummax(jnp.where(begin_mask, frame_idx, -1).astype(jnp.int32), axis=1)
    ahead_idx = jnp.where(begin_mask, frame_idx, GROUP_FR).astype(jnp.int32)
    after_idx = lax.cummin(ahead_idx, axis=1, reverse=True)
    stop_idx = jnp.concatenate([after_idx[:, 1:], jnp.full((N_GRP, 1), GROUP_FR, jnp.int32)], axis=1)
    return (start_idx, stop_idx)

def layer_norm(hidden, norm_gain):
    values = hidden.astype(jnp.float32)
    centred = values - lax.optimization_barrier(jnp.mean(values, axis=-1, keepdims=True))
    spread = lax.optimization_barrier(jnp.mean(centred * centred, axis=-1, keepdims=True))
    return (centred * lax.rsqrt(spread + 1e-05) * norm_gain).astype(jnp.bfloat16)

def attend_group(queries, keyval, start_idx, stop_idx):
    left_reach = (LEFT_BLOCKS + 1) * BLOCK_LEN
    right_reach = BLOCK_LEN
    span = 512 + left_reach + right_reach
    padded_kv = jnp.pad(keyval, ((left_reach, right_reach), (0, 0)))

    def one_block(block_id):
        base = (block_id * 512).astype(jnp.int32)
        query_rows = lax.dynamic_slice(queries, (base, jnp.int32(0)), (512, D))
        key_rows = lax.dynamic_slice(padded_kv, (base, jnp.int32(0)), (span, 2 * D))
        first = lax.dynamic_slice(start_idx, (base,), (512,))
        last = lax.dynamic_slice(stop_idx, (base,), (512,))
        query_idx = base + jnp.arange(512, dtype=jnp.int32)
        key_idx = base - left_reach + jnp.arange(span, dtype=jnp.int32)
        query_block = (query_idx - first) // BLOCK_LEN
        key_block = (key_idx[None, :] - first[:, None]) // BLOCK_LEN
        allowed = (key_idx[None, :] >= first[:, None]) & (key_idx[None, :] < last[:, None])
        allowed = allowed & (key_block >= query_block[:, None] - LEFT_BLOCKS) & (key_block <= query_block[:, None])
        query_heads = query_rows.astype(jnp.float32).reshape(512, HEADS, HEAD_DIM)
        key_heads = key_rows[:, :D].astype(jnp.float32).reshape(span, HEADS, HEAD_DIM)
        value_heads = key_rows[:, D:].astype(jnp.float32).reshape(span, HEADS, HEAD_DIM)
        scores = jnp.einsum('qhd,khd->hqk', query_heads, key_heads) / jnp.sqrt(jnp.float32(HEAD_DIM))
        scores = jnp.where(allowed[None], scores, jnp.float32(-1e+30))
        top = lax.optimization_barrier(jnp.max(scores, axis=-1, keepdims=True))
        expo = jnp.exp(scores - top)
        weights = (expo / lax.optimization_barrier(jnp.sum(expo, axis=-1, keepdims=True))).astype(jnp.bfloat16)
        mixed = jnp.einsum('hqk,khd->qhd', weights.astype(jnp.float32), value_heads)
        return mixed.reshape(512, D).astype(jnp.bfloat16)
    blocks = lax.map(one_block, jnp.arange(GROUP_FR // 512, dtype=jnp.int32))
    return blocks.reshape(GROUP_FR, D)

def reference(frames, begins, owner, conv_kernel, norm_gain, w_qkv, w_out, cotangent):
    start_idx, stop_idx = utterance_bounds(begins)
    frame_idx = jnp.arange(GROUP_FR, dtype=jnp.int32)[None, :]
    reach = KERNEL // 2
    padded = jnp.pad(frames, ((0, 0), (reach, reach), (0, 0)))
    conv_sum = jnp.zeros((N_GRP, GROUP_FR, D), jnp.float32)
    for tap in range(KERNEL):
        source_idx = frame_idx + tap - reach
        inside = (source_idx >= start_idx) & (source_idx < stop_idx)
        term = padded[:, tap:tap + GROUP_FR].astype(jnp.float32) * conv_kernel[tap]
        conv_sum = conv_sum + jnp.where(inside[:, :, None], term, jnp.float32(0.0))
    hidden = (frames.astype(jnp.float32) + conv_sum).astype(jnp.bfloat16)
    normed = layer_norm(hidden, norm_gain).reshape(N_GRP * GROUP_FR, D)
    qkv = jnp.dot(normed, w_qkv, preferred_element_type=jnp.float32).astype(jnp.bfloat16)
    qkv = qkv.reshape(N_GRP, GROUP_FR, 3 * D)
    attn = jnp.stack([attend_group(qkv[g, :, :D], qkv[g, :, D:], start_idx[g], stop_idx[g]) for g in range(N_GRP)])
    projected = jnp.dot(attn.reshape(N_GRP * GROUP_FR, D), w_out, preferred_element_type=jnp.float32)
    outputs = hidden.astype(jnp.float32) + projected.reshape(N_GRP, GROUP_FR, D)
    pooled = lax.optimization_barrier(jnp.mean(outputs.reshape(N_GRP, GROUP_ROWS, SUB, D), axis=2)).astype(jnp.bfloat16)
    destination = owner[:, :, 0].reshape(N_GRP, N_SEQ, ROWS_DEV)
    onehot = (destination[..., None] == jnp.arange(N_SEQ, dtype=jnp.int32)).astype(jnp.int32)
    before = jnp.cumsum(onehot, axis=2) - onehot
    rank_index = lax.optimization_barrier(jnp.sum(onehot * before, axis=-1))
    source = jnp.arange(N_SEQ, dtype=jnp.int32)[None, :, None]
    slot_index = (destination * OWN_SLOTS + source * CAP + rank_index).reshape(N_GRP, GROUP_ROWS).astype(jnp.int32)
    group_ids = jnp.arange(N_GRP, dtype=jnp.int32)[:, None]
    audio_rows = jnp.zeros((N_GRP, N_SEQ * OWN_SLOTS, D), jnp.bfloat16).at[group_ids, slot_index].set(pooled)
    row_grads = cotangent[group_ids, slot_index].astype(jnp.float32)
    pooled_attn = lax.optimization_barrier(jnp.sum(attn.astype(jnp.float32).reshape(N_GRP, GROUP_ROWS, SUB, D), axis=2))
    grad_total = jnp.einsum('grd,gre->de', pooled_attn, row_grads / SUB, precision=lax.Precision.HIGHEST)
    out_grad = (grad_total / jnp.sqrt(jnp.float32(N_GRP * GROUP_ROWS))).astype(jnp.bfloat16)
    return (audio_rows, out_grad)
```

```python
import jax
import jax.numpy as jnp
from jax import lax
from jax.experimental import pallas as pl
from jax.experimental.pallas import tpu as pltpu
from jax.sharding import PartitionSpec as P

HEADS = 8
BLOCK_LEN = 32
LEFT_BLOCKS = 2
SUB = 8
F = 512
D = 1024
LEFT = 112
RIGHT = 48
KV = 640
KOFF = 96
FAR = 1536
BIG = 1e6
F32 = jnp.float32
BF16 = jnp.bfloat16


def bounds(bg, t0, group_len, dprev, dnext):
    lanes = FAR + F + 128
    u = lax.broadcasted_iota(jnp.int32, (1, lanes), 1) - FAR
    at = u + t0
    mark = ((bg == 1) & (at >= 0)) | (at == group_len)
    uf = u.astype(F32)
    last = jnp.where(mark, uf, -BIG)
    early = jnp.max(last[:, : FAR - 128], axis=1, keepdims=True)
    near_last = last[:, FAR - 128 :]
    near_first = jnp.where(mark, uf, BIG)[:, FAR - 128 :]
    near = uf[:, FAR - 128 :]
    for c in range(KV // 128):
        t = (lax.broadcasted_iota(jnp.int32, (128, 1), 0) + (128 * c - KOFF)).astype(F32)
        before = near <= t
        start = jnp.max(jnp.where(before, near_last, -BIG), axis=1, keepdims=True)
        start = jnp.maximum(start, early)
        stop = jnp.min(jnp.where(before, BIG, near_first), axis=1, keepdims=True)
        dprev[128 * c : 128 * c + 128, :] = jnp.broadcast_to(t - start, (128, 128))
        dnext[128 * c : 128 * c + 128, :] = jnp.broadcast_to(stop - t, (128, 128))


def attention_bias(dprev, dnext, bias):
    for i in range(F // 128):
        rows = slice(KOFF + 128 * i, KOFF + 128 * i + 128)
        back = dprev[rows, :].astype(jnp.int32)
        ahead = dnext[rows, :].astype(jnp.int32)
        rem = back & (BLOCK_LEN - 1)
        low = -jnp.minimum(back, rem + LEFT_BLOCKS * BLOCK_LEN)
        high = jnp.minimum(ahead, BLOCK_LEN - rem)
        for half in range(2):
            delta = (
                lax.broadcasted_iota(jnp.int32, (128, 128), 1)
                - lax.broadcasted_iota(jnp.int32, (128, 128), 0)
                + (128 * half - KOFF)
            )
            ok = (delta >= low) & (delta < high)
            bias[i, :, 128 * half : 128 * half + 128] = jnp.where(ok, F32(0.0), F32(-1e30))


def conv_norm(xf, taps, gain, dprev, dnext, hid, nrm):
    step = 32
    tiles = D // 128

    def block(n, _):
        r0 = pl.multiple_of(n * step, step)
        back = dprev[pl.ds(r0, step), :]
        ahead = dnext[pl.ds(r0, step), :]
        keep = [back >= F32(4 - j) if j < 4 else ahead > F32(j - 4) for j in range(9)]
        hs = []
        total = jnp.zeros((step, 128), F32)
        for c in range(tiles):
            cols = slice(128 * c, 128 * c + 128)
            centre = xf[c, pl.ds(r0 + 16, step), :]
            acc = centre * taps[4:5, cols]
            for j in range(9):
                if j == 4:
                    continue
                term = xf[c, pl.ds(r0 + 12 + j, step), :] * taps[j : j + 1, cols]
                acc = acc + jnp.where(keep[j], term, F32(0.0))
            h16 = (centre + acc).astype(BF16)
            hid[pl.ds(r0, step), cols] = h16
            h = h16.astype(F32)
            hs.append(h)
            total = total + h
        mean = jnp.sum(total, axis=1, keepdims=True) * F32(1.0 / D)
        hs = [h - mean for h in hs]
        square = jnp.zeros((step, 128), F32)
        for h in hs:
            square = square + h * h
        var = jnp.sum(square, axis=1, keepdims=True) * F32(1.0 / D)
        scale = lax.rsqrt(var + F32(1e-5))
        for c in range(tiles):
            cols = slice(128 * c, 128 * c + 128)
            nrm[pl.ds(r0, step), cols] = (hs[c] * scale * gain[:, cols]).astype(BF16)
        return 0

    lax.fori_loop(0, KV // step, block, 0)


def attend(nrm, wqkv, bias, qs, ks, vs, attn):
    factor = F32(1.4426950408889634 / 128.0**0.5)

    def pair(hp, _):
        def cols(base):
            return pl.ds(pl.multiple_of(base + hp * 256, 256), 256)

        qs[...] = jnp.dot(
            nrm[KOFF : KOFF + F, :], wqkv[:, cols(0)], preferred_element_type=F32
        ).astype(BF16)
        ks[...] = jnp.dot(nrm[...], wqkv[:, cols(D)], preferred_element_type=F32).astype(BF16)
        vs[...] = jnp.dot(nrm[...], wqkv[:, cols(2 * D)], preferred_element_type=F32).astype(BF16)
        for hh in range(2):
            lanes = slice(128 * hh, 128 * hh + 128)
            for i in range(F // 128):
                q = qs[128 * i : 128 * i + 128, lanes]
                k = ks[128 * i : 128 * i + 256, lanes]
                v = vs[128 * i : 128 * i + 256, lanes]
                s = lax.dot_general(q, k, (((1,), (1,)), ((), ())), preferred_element_type=F32)
                s = s + bias[i]
                top = jnp.max(s, axis=1, keepdims=True)
                e = jnp.exp2((s - top) * factor)
                norm = F32(1.0) / jnp.sum(e, axis=1, keepdims=True)
                w = (e * norm).astype(BF16)
                o = jnp.dot(w, v, preferred_element_type=F32).astype(BF16)
                attn[
                    128 * i : 128 * i + 128,
                    pl.ds(pl.multiple_of(hp * 256 + 128 * hh, 128), 128),
                ] = o
        return 0

    lax.fori_loop(0, HEADS // 2, pair, 0)


def placement_of(owner):
    rows = owner.shape[0]
    lane = lax.broadcasted_iota(jnp.int32, (rows, 128), 1)
    hot = jnp.where(owner == lane, F32(1.0), F32(0.0))
    lower = jnp.where(
        lax.broadcasted_iota(jnp.int32, (rows, rows), 1)
        < lax.broadcasted_iota(jnp.int32, (rows, rows), 0),
        F32(1.0),
        F32(0.0),
    ).astype(BF16)
    before = jnp.dot(lower, hot.astype(BF16), preferred_element_type=F32)
    rank = jnp.sum(hot * before, axis=1, keepdims=True).astype(jnp.int32)
    slot = owner * 4 + rank
    return jnp.where(slot == lane, F32(1.0), F32(0.0)).astype(BF16)


def pool(hid, attn, wout):
    rows = F // SUB
    gather = jnp.where(
        lax.broadcasted_iota(jnp.int32, (rows, F), 1) >> 3
        == lax.broadcasted_iota(jnp.int32, (rows, F), 0),
        F32(1.0),
        F32(0.0),
    ).astype(BF16)
    asum = jnp.dot(gather, attn[...], preferred_element_type=F32)
    hsum = jnp.dot(gather, hid[KOFF : KOFF + F, :], preferred_element_type=F32)
    high = asum.astype(BF16)
    low = (asum - high.astype(F32)).astype(BF16)
    proj = jnp.dot(high, wout[...], preferred_element_type=F32)
    proj = proj + jnp.dot(low, wout[...], preferred_element_type=F32)
    pooled = ((hsum + proj) * F32(1.0 / SUB)).astype(BF16)
    return pooled, high, low


def local_kernel(
    x_hbm, bg_ref, owner_ref, taps_ref, gain_ref, wqkv_hbm, wout_hbm,
    out_ref, place_ref, a_ref,
    xb, xf, dprev, dnext, hid, nrm, qs, ks, vs, bias, attn, wqkv, wout, sems,
):
    cx = pltpu.make_async_copy(x_hbm, xb, sems.at[0])
    cq = pltpu.make_async_copy(wqkv_hbm, wqkv, sems.at[1])
    co = pltpu.make_async_copy(wout_hbm, wout, sems.at[2])
    cx.start()
    cq.start()
    co.start()
    t0 = lax.axis_index("seq") * F
    bounds(bg_ref[...], t0, F * lax.axis_size("seq"), dprev, dnext)
    attention_bias(dprev, dnext, bias)
    place = placement_of(owner_ref[...])
    place_ref[...] = place
    cx.wait()
    for c in range(D // 128):
        xf[c] = xb[:, 128 * c : 128 * c + 128].astype(F32)
    conv_norm(xf, taps_ref, gain_ref, dprev, dnext, hid, nrm)
    cq.wait()
    attend(nrm, wqkv, bias, qs, ks, vs, attn)
    co.wait()
    pooled, high, low = pool(hid, attn, wout)
    a_ref[0] = high
    a_ref[1] = low
    out_ref[...] = lax.dot_general(
        place, pooled, (((0,), (0,)), ((), ())), preferred_element_type=F32
    ).astype(BF16)


def shards(frames, begins, owner, conv_kernel, norm_gain, w_qkv, w_out, cotangent):
    n = lax.axis_size("seq")
    shift = lambda a, by: lax.ppermute(a, "seq", [(i, (i + by) % n) for i in range(n)])
    x = jnp.concatenate(
        [shift(frames[0, F - LEFT :], 1), frames[0], shift(frames[0, :RIGHT], -1)], axis=0
    )
    bg = jnp.concatenate(
        [shift(begins, 3), shift(begins, 2), shift(begins, 1), begins, shift(begins[:, :128], -1)],
        axis=1,
    )
    vm = pl.BlockSpec(memory_space=pltpu.VMEM)
    hbm = pl.BlockSpec(memory_space=pl.ANY)
    outgoing, place, asum = pl.pallas_call(
        local_kernel,
        out_shape=(
            jax.ShapeDtypeStruct((128, D), BF16),
            jax.ShapeDtypeStruct((64, 128), BF16),
            jax.ShapeDtypeStruct((2, 64, D), BF16),
        ),
        in_specs=[hbm, vm, vm, vm, vm, hbm, hbm],
        out_specs=(vm, vm, vm),
        scratch_shapes=[
            pltpu.VMEM((LEFT + F + RIGHT, D), BF16),
            pltpu.VMEM((8, LEFT + F + RIGHT, 128), F32),
            pltpu.VMEM((KV, 128), F32),
            pltpu.VMEM((KV, 128), F32),
            pltpu.VMEM((KV, D), BF16),
            pltpu.VMEM((KV, D), BF16),
            pltpu.VMEM((F, 256), BF16),
            pltpu.VMEM((KV, 256), BF16),
            pltpu.VMEM((KV, 256), BF16),
            pltpu.VMEM((4, 128, 256), F32),
            pltpu.VMEM((F, D), BF16),
            pltpu.VMEM((D, 3 * D), BF16),
            pltpu.VMEM((D, D), BF16),
            pltpu.SemaphoreType.DMA((3,)),
        ],
        compiler_params=pltpu.CompilerParams(vmem_limit_bytes=48 * 1024 * 1024),
        name="local",
    )(x, bg, owner[0], conv_kernel, norm_gain.reshape(1, D), w_qkv, w_out)
    incoming = lax.all_to_all(outgoing.reshape(n, 4, D), "seq", 0, 0, tiled=True)
    returned = lax.all_to_all(cotangent[0].reshape(n, 4, D), "seq", 0, 0, tiled=True)
    grads = jnp.dot(place, returned.reshape(128, D), preferred_element_type=F32).astype(BF16)
    dims = (((0,), (0,)), ((), ()))
    local = lax.dot_general(asum[0], grads, dims, preferred_element_type=F32)
    local = local + lax.dot_general(asum[1], grads, dims, preferred_element_type=F32)
    total = lax.psum(local * F32(1.0 / (8 * 128)), ("grp", "seq"))
    return incoming.reshape(1, 128, D), total.astype(BF16)


def solution(mesh):
    return jax.shard_map(
        shards,
        mesh=mesh,
        in_specs=(
            P("grp", "seq", None),
            P("grp", "seq"),
            P("grp", "seq", None),
            P(),
            P(),
            P(),
            P(),
            P("grp", "seq", None),
        ),
        out_specs=(P("grp", "seq", None), P()),
        check_vma=False,
    )
```

```python
import jax
import jax.numpy as jnp
from jax import lax
from jax.experimental import pallas as pl
from jax.experimental.pallas import tpu as pltpu
from jax.sharding import PartitionSpec as P

HEADS = 8
BLOCK_LEN = 32
LEFT_BLOCKS = 2
SUB = 8
F = 512
D = 1024
LEFT = 112
RIGHT = 48
KV = 640
KOFF = 96
FAR = 1536
BIG = 1e6
F32 = jnp.float32
BF16 = jnp.bfloat16
MESH = pl.DeviceIdType.MESH
N_SEQ = 32
N_GRP = 8
N_X = 4
N_Y = 4
GROUP = 8


def bounds(bg, t0, group_len, dprev, dnext):
    lanes = FAR + F + 128
    u = lax.broadcasted_iota(jnp.int32, (1, lanes), 1) - FAR
    at = u + t0
    mark = ((bg == 1) & (at >= 0)) | (at == group_len)
    uf = u.astype(F32)
    last = jnp.where(mark, uf, -BIG)
    early = jnp.max(last[:, : FAR - 128], axis=1, keepdims=True)
    near_last = last[:, FAR - 128 :]
    near_first = jnp.where(mark, uf, BIG)[:, FAR - 128 :]
    near = uf[:, FAR - 128 :]
    for c in range(KV // 128):
        t = (lax.broadcasted_iota(jnp.int32, (128, 1), 0) + (128 * c - KOFF)).astype(F32)
        before = near <= t
        start = jnp.max(jnp.where(before, near_last, -BIG), axis=1, keepdims=True)
        start = jnp.maximum(start, early)
        stop = jnp.min(jnp.where(before, BIG, near_first), axis=1, keepdims=True)
        dprev[128 * c : 128 * c + 128, :] = jnp.broadcast_to(t - start, (128, 128))
        dnext[128 * c : 128 * c + 128, :] = jnp.broadcast_to(stop - t, (128, 128))


def attention_bias(dprev, dnext, bias):
    for i in range(F // 128):
        rows = slice(KOFF + 128 * i, KOFF + 128 * i + 128)
        back = dprev[rows, :].astype(jnp.int32)
        ahead = dnext[rows, :].astype(jnp.int32)
        rem = back & (BLOCK_LEN - 1)
        low = -jnp.minimum(back, rem + LEFT_BLOCKS * BLOCK_LEN)
        high = jnp.minimum(ahead, BLOCK_LEN - rem)
        for half in range(2):
            delta = (
                lax.broadcasted_iota(jnp.int32, (128, 128), 1)
                - lax.broadcasted_iota(jnp.int32, (128, 128), 0)
                + (128 * half - KOFF)
            )
            ok = (delta >= low) & (delta < high)
            bias[i, :, 128 * half : 128 * half + 128] = jnp.where(ok, F32(0.0), F32(-1e30))


def conv_norm(xf, taps, gain, dprev, dnext, hid, nrm):
    step = 32
    tiles = D // 128

    def block(n, _):
        r0 = pl.multiple_of(n * step, step)
        back = dprev[pl.ds(r0, step), :]
        ahead = dnext[pl.ds(r0, step), :]
        keep = [back >= F32(4 - j) if j < 4 else ahead > F32(j - 4) for j in range(9)]
        hs = []
        total = jnp.zeros((step, 128), F32)
        for c in range(tiles):
            cols = slice(128 * c, 128 * c + 128)
            centre = xf[c, pl.ds(r0 + 16, step), :]
            acc = centre * taps[4:5, cols]
            for j in range(9):
                if j == 4:
                    continue
                term = xf[c, pl.ds(r0 + 12 + j, step), :] * taps[j : j + 1, cols]
                acc = acc + jnp.where(keep[j], term, F32(0.0))
            h16 = (centre + acc).astype(BF16)
            hid[pl.ds(r0, step), cols] = h16
            h = h16.astype(F32)
            hs.append(h)
            total = total + h
        mean = jnp.sum(total, axis=1, keepdims=True) * F32(1.0 / D)
        hs = [h - mean for h in hs]
        square = jnp.zeros((step, 128), F32)
        for h in hs:
            square = square + h * h
        var = jnp.sum(square, axis=1, keepdims=True) * F32(1.0 / D)
        scale = lax.rsqrt(var + F32(1e-5))
        for c in range(tiles):
            cols = slice(128 * c, 128 * c + 128)
            nrm[pl.ds(r0, step), cols] = (hs[c] * scale * gain[:, cols]).astype(BF16)
        return 0

    lax.fori_loop(0, KV // step, block, 0)


def attend(nrm, wqkv, bias, qs, ks, vs, attn):
    factor = F32(1.4426950408889634 / 128.0**0.5)

    def pair(hp, _):
        def cols(base):
            return pl.ds(pl.multiple_of(base + hp * 256, 256), 256)

        qs[...] = jnp.dot(
            nrm[KOFF : KOFF + F, :], wqkv[:, cols(0)], preferred_element_type=F32
        ).astype(BF16)
        ks[...] = jnp.dot(nrm[...], wqkv[:, cols(D)], preferred_element_type=F32).astype(BF16)
        vs[...] = jnp.dot(nrm[...], wqkv[:, cols(2 * D)], preferred_element_type=F32).astype(BF16)
        for hh in range(2):
            lanes = slice(128 * hh, 128 * hh + 128)
            for i in range(F // 128):
                q = qs[128 * i : 128 * i + 128, lanes]
                k = ks[128 * i : 128 * i + 256, lanes]
                v = vs[128 * i : 128 * i + 256, lanes]
                s = lax.dot_general(q, k, (((1,), (1,)), ((), ())), preferred_element_type=F32)
                s = s + bias[i]
                top = jnp.max(s, axis=1, keepdims=True)
                e = jnp.exp2((s - top) * factor)
                norm = F32(1.0) / jnp.sum(e, axis=1, keepdims=True)
                w = (e * norm).astype(BF16)
                o = jnp.dot(w, v, preferred_element_type=F32).astype(BF16)
                attn[
                    128 * i : 128 * i + 128,
                    pl.ds(pl.multiple_of(hp * 256 + 128 * hh, 128), 128),
                ] = o
        return 0

    lax.fori_loop(0, HEADS // 2, pair, 0)


def placement_of(owner):
    rows = owner.shape[0]
    lane = lax.broadcasted_iota(jnp.int32, (rows, 128), 1)
    hot = jnp.where(owner == lane, F32(1.0), F32(0.0))
    lower = jnp.where(
        lax.broadcasted_iota(jnp.int32, (rows, rows), 1)
        < lax.broadcasted_iota(jnp.int32, (rows, rows), 0),
        F32(1.0),
        F32(0.0),
    ).astype(BF16)
    before = jnp.dot(lower, hot.astype(BF16), preferred_element_type=F32)
    rank = jnp.sum(hot * before, axis=1, keepdims=True).astype(jnp.int32)
    slot = owner * 4 + rank
    return jnp.where(slot == lane, F32(1.0), F32(0.0)).astype(BF16)


def remote(src, dst, sends, recvs, index, target):
    return pltpu.make_async_remote_copy(
        src_ref=src,
        dst_ref=dst,
        send_sem=sends.at[index],
        recv_sem=recvs.at[index],
        device_id=target,
        device_id_type=MESH,
    )


def each(count, body):
    def one(k, _):
        body(k)
        return 0

    lax.fori_loop(1, count, one, 0)


def to_slots(value, wide, slots):
    for c in range(D // 128):
        wide[pl.ds(c, 128, stride=8), :] = value[:, 128 * c : 128 * c + 128].astype(F32)
    for o in range(N_SEQ):
        slots[o] = wide[32 * o : 32 * o + 32, :].astype(BF16)


def from_slots(slots, wide):
    for o in range(N_SEQ):
        wide[32 * o : 32 * o + 32, :] = slots[o].astype(F32)
    return [wide[pl.ds(c, 128, stride=8), :].astype(BF16) for c in range(D // 128)]


def whole_kernel(
    frames, begins, owner, taps, gain, wqkv_hbm, wout_hbm, cot_hbm,
    audio, fin,
    xb, xf, bgs, dprev, dnext, hid, nrm, qs, ks, vs, bias, attn, wqkv, wout,
    cotv, cots, back, wide, gall, asp, aall, part, xr, quarter, zr, aout,
    local_sems, halo_s, halo_r, cot_s, cot_r, g_s, g_r, a_s, a_r, x_s, x_r, z_s, z_r,
    t_s, t_r, m_s, m_r, h0_s, h0_r, h1_s, h1_r, p0_s, p0_r, p1_s, p1_r, c_s, c_r,
):
    z = lax.axis_index("grp")
    s = lax.axis_index("seq")
    x = s // GROUP
    j = s % GROUP
    y = j // 2
    c = j % 2

    def seq(k):
        return {"seq": (s + k) % N_SEQ}

    def grp(k):
        return {"grp": (z + k) % N_GRP}

    def in_group(k):
        return {"seq": x * GROUP + (j + k) % GROUP}

    def along_x(k):
        return {"seq": (x + k) % N_X * GROUP + j}

    def along_y(k):
        return {"seq": x * GROUP + (y + k) % N_Y * 2 + c}

    other_core = {"seq": x * GROUP + y * 2 + (1 - c)}

    barrier = pltpu.get_barrier_semaphore()

    def greet(target):
        pl.semaphore_signal(barrier, inc=1, device_id=target, device_id_type=MESH)

    each(N_SEQ, lambda k: greet(seq(k)))
    each(N_GRP, lambda k: greet(grp(k)))

    loads = [
        pltpu.make_async_copy(cot_hbm.at[0], cotv, local_sems.at[0]),
        pltpu.make_async_copy(begins, bgs.at[3], local_sems.at[1]),
        pltpu.make_async_copy(frames.at[0], xb.at[pl.ds(LEFT, F)], local_sems.at[2]),
        pltpu.make_async_copy(wqkv_hbm, wqkv, local_sems.at[3]),
        pltpu.make_async_copy(wout_hbm, wout, local_sems.at[4]),
    ]
    for copy in loads:
        copy.start()
    loads[0].wait()
    to_slots(cotv[...], wide, cots)
    place = placement_of(owner[...])

    pl.semaphore_wait(barrier, N_SEQ - 1 + N_GRP - 1)

    halo = [
        remote(frames.at[0, pl.ds(F - LEFT, LEFT)], xb.at[pl.ds(0, LEFT)], halo_s, halo_r, 0, seq(1)),
        remote(frames.at[0, pl.ds(0, RIGHT)], xb.at[pl.ds(LEFT + F, RIGHT)], halo_s, halo_r, 1, seq(N_SEQ - 1)),
        remote(begins, bgs.at[2], halo_s, halo_r, 2, seq(1)),
        remote(begins, bgs.at[1], halo_s, halo_r, 3, seq(2)),
        remote(begins, bgs.at[0], halo_s, halo_r, 4, seq(3)),
        remote(begins, bgs.at[4], halo_s, halo_r, 5, seq(N_SEQ - 1)),
    ]
    for copy in halo[2:] + halo[:2]:
        copy.start()

    def send_cot(k):
        remote(cots.at[(s + k) % N_SEQ], back.at[s], cot_s, cot_r, k, seq(k)).start()

    each(N_SEQ, send_cot)
    back[s] = cots[s]

    loads[1].wait()
    for copy in halo[2:]:
        copy.wait_recv()
    marks = jnp.concatenate([bgs[0], bgs[1], bgs[2], bgs[3], bgs[4][:, :128]], axis=1)
    bounds(marks, s * F, F * N_SEQ, dprev, dnext)
    attention_bias(dprev, dnext, bias)
    loads[2].wait()
    for copy in halo[:2]:
        copy.wait_recv()
    for tile in range(D // 128):
        xf[tile] = xb[:, 128 * tile : 128 * tile + 128].astype(F32)
    conv_norm(xf, taps, gain, dprev, dnext, hid, nrm)

    def got_cot(k):
        source = (s + N_SEQ - k) % N_SEQ
        remote(back.at[source], back.at[source], cot_s, cot_r, k, seq(k)).wait_recv()

    each(N_SEQ, got_cot)
    mine = pl.ds(pl.multiple_of(j * 64, 64), 64)
    returned = from_slots(back, wide)
    for tile in range(D // 128):
        gall[mine, 128 * tile : 128 * tile + 128] = jnp.dot(
            place, returned[tile], preferred_element_type=F32
        ).astype(BF16)

    def copy_g(k):
        return remote(gall.at[mine], gall.at[mine], g_s, g_r, k, in_group(k))

    each(GROUP, lambda k: copy_g(k).start())

    loads[3].wait()
    attend(nrm, wqkv, bias, qs, ks, vs, attn)
    rows = F // SUB
    gather = jnp.where(
        lax.broadcasted_iota(jnp.int32, (rows, F), 1) >> 3
        == lax.broadcasted_iota(jnp.int32, (rows, F), 0),
        F32(1.0),
        F32(0.0),
    ).astype(BF16)
    asum = jnp.dot(gather, attn[...], preferred_element_type=F32)
    high = asum.astype(BF16)
    low = (asum - high.astype(F32)).astype(BF16)
    for h in range(HEADS):
        asp[h, 0] = high[:, 128 * h : 128 * h + 128]
        asp[h, 1] = low[:, 128 * h : 128 * h + 128]

    def copy_a(k):
        return remote(asp.at[(j + k) % GROUP], aall.at[:, mine, :], a_s, a_r, k, in_group(k))

    each(GROUP, lambda k: copy_a(k).start())
    aall[:, mine, :] = asp[j]

    loads[4].wait()
    hsum = jnp.dot(gather, hid[KOFF : KOFF + F, :], preferred_element_type=F32)
    proj = jnp.dot(high, wout[...], preferred_element_type=F32)
    proj = proj + jnp.dot(low, wout[...], preferred_element_type=F32)
    pooled = ((hsum + proj) * F32(1.0 / SUB)).astype(BF16)
    dims = (((0,), (0,)), ((), ()))
    outgoing = lax.dot_general(place, pooled, dims, preferred_element_type=F32)
    to_slots(outgoing, wide, aout)

    def copy_audio(k):
        return remote(aout.at[(s + k) % N_SEQ], audio.at[s], m_s, m_r, k, seq(k))

    each(N_SEQ, lambda k: copy_audio(k).start())
    audio[s] = aout[s]

    each(GROUP, lambda k: copy_g(k).wait_recv())
    each(GROUP, lambda k: copy_a(k).wait_recv())
    part[...] = lax.dot_general(aall[0], gall[...], dims, preferred_element_type=F32)
    part[...] += lax.dot_general(aall[1], gall[...], dims, preferred_element_type=F32)

    def rows_of(place_x):
        return pl.ds(pl.multiple_of(place_x * 32, 32), 32)

    def copy_x(k):
        return remote(part.at[rows_of((x + k) % N_X)], xr.at[k], x_s, x_r, k, along_x(k))

    for k in range(1, N_X):
        copy_x(k).start()
    for k in range(1, N_X):
        copy_x(k).wait_recv()
    total = part[rows_of(x), :] + xr[1] + xr[2] + xr[3]
    for tile in range(N_GRP):
        quarter[tile] = total[:, 128 * tile : 128 * tile + 128]

    def copy_z(k):
        return remote(quarter.at[(z + k) % N_GRP], zr.at[k], z_s, z_r, k, grp(k))

    for k in range(1, N_GRP):
        copy_z(k).start()
    for k in range(1, N_GRP):
        copy_z(k).wait_recv()
    tile_sum = quarter[z]
    for k in range(1, N_GRP):
        tile_sum = tile_sum + zr[k]
    own_cols = pl.ds(pl.multiple_of(z * 128, 128), 128)
    fin[y, c, x, :, own_cols] = (tile_sum * F32(1.0 / (128 * SUB))).astype(BF16)

    def copy_t(k):
        tile = fin.at[y, c, x, :, own_cols]
        return remote(tile, tile, t_s, t_r, k, grp(k))

    for k in range(1, N_GRP):
        copy_t(k).start()
    for k in range(1, N_GRP):
        copy_t(k).wait_recv()

    first, second = pl.ds(0, D // 2), pl.ds(D // 2, D // 2)

    def copy_h0(k):
        block = fin.at[y, c, x, :, first]
        return remote(block, block, h0_s, h0_r, k, along_x(k))

    def copy_h1(k):
        block = fin.at[y, c, x, :, second]
        return remote(block, block, h1_s, h1_r, k, along_y(k))

    def copy_p0(k):
        block = fin.at[y, c, :, :, first]
        return remote(block, block, p0_s, p0_r, k, along_y(k))

    def copy_p1(k):
        block = fin.at[:, c, x, :, second]
        return remote(block, block, p1_s, p1_r, k, along_x(k))

    def copy_c0(k):
        block = fin.at[(y + N_Y - k) % N_Y, c, :, :, first]
        return remote(block, block, c_s, c_r, k, other_core)

    def copy_c1(k):
        block = fin.at[:, c, (x + N_X - k) % N_X, :, second]
        return remote(block, block, c_s, c_r, N_Y + k, other_core)

    for k in range(1, N_X):
        copy_h0(k).start()
        copy_h1(k).start()
    for k in range(1, N_X):
        copy_h0(k).wait_recv()
    for k in range(1, N_Y):
        copy_p0(k).start()
    copy_c0(0).start()
    for k in range(1, N_Y):
        copy_h1(k).wait_recv()
    for k in range(1, N_X):
        copy_p1(k).start()
    copy_c1(0).start()
    for k in (1, 3, 2):
        copy_p0(k).wait_recv()
        copy_c0(k).start()
        copy_p1(k).wait_recv()
        copy_c1(k).start()
    for k in range(N_Y):
        copy_c0(k).wait_recv()
        copy_c1(k).wait_recv()

    def got_audio(k):
        source = (s + N_SEQ - k) % N_SEQ
        remote(audio.at[source], audio.at[source], m_s, m_r, k, seq(k)).wait_recv()

    each(N_SEQ, got_audio)
    for copy in halo:
        copy.wait_send()

    def sent(k):
        remote(cots.at[(s + k) % N_SEQ], back.at[s], cot_s, cot_r, k, seq(k)).wait_send()
        copy_audio(k).wait_send()

    each(N_SEQ, sent)

    def sent_group(k):
        copy_g(k).wait_send()
        copy_a(k).wait_send()
        copy_z(k).wait_send()
        copy_t(k).wait_send()

    each(GROUP, sent_group)
    for k in range(1, N_X):
        copy_x(k).wait_send()
        copy_h0(k).wait_send()
        copy_h1(k).wait_send()
        copy_p0(k).wait_send()
        copy_p1(k).wait_send()
    for k in range(N_Y):
        copy_c0(k).wait_send()
        copy_c1(k).wait_send()


def shards(frames, begins, owner, conv_kernel, norm_gain, w_qkv, w_out, cotangent):
    vm = pl.BlockSpec(memory_space=pltpu.VMEM)
    hbm = pl.BlockSpec(memory_space=pl.ANY)
    dma = pltpu.SemaphoreType.DMA
    audio, grad = pl.pallas_call(
        whole_kernel,
        out_shape=(
            jax.ShapeDtypeStruct((N_SEQ, 32, 128), BF16),
            jax.ShapeDtypeStruct((N_Y, 2, N_X, 32, D), BF16),
        ),
        in_specs=[hbm, hbm, vm, vm, vm, hbm, hbm, hbm],
        out_specs=(vm, vm),
        scratch_shapes=[
            pltpu.VMEM((LEFT + F + RIGHT, D), BF16),
            pltpu.VMEM((8, LEFT + F + RIGHT, 128), F32),
            pltpu.VMEM((5, 1, F), jnp.int32),
            pltpu.VMEM((KV, 128), F32),
            pltpu.VMEM((KV, 128), F32),
            pltpu.VMEM((KV, D), BF16),
            pltpu.VMEM((KV, D), BF16),
            pltpu.VMEM((F, 256), BF16),
            pltpu.VMEM((KV, 256), BF16),
            pltpu.VMEM((KV, 256), BF16),
            pltpu.VMEM((4, 128, 256), F32),
            pltpu.VMEM((F, D), BF16),
            pltpu.VMEM((D, 3 * D), BF16),
            pltpu.VMEM((D, D), BF16),
            pltpu.VMEM((128, D), BF16),
            pltpu.VMEM((N_SEQ, 32, 128), BF16),
            pltpu.VMEM((N_SEQ, 32, 128), BF16),
            pltpu.VMEM((1024, 128), F32),
            pltpu.VMEM((512, D), BF16),
            pltpu.VMEM((HEADS, 2, 64, 128), BF16),
            pltpu.VMEM((2, 512, 128), BF16),
            pltpu.VMEM((128, D), F32),
            pltpu.VMEM((N_X, 32, D), F32),
            pltpu.VMEM((N_GRP, 32, 128), F32),
            pltpu.VMEM((N_GRP, 32, 128), F32),
            pltpu.VMEM((N_SEQ, 32, 128), BF16),
            dma((5,)),
            dma((6,)), dma((6,)),
            dma((N_SEQ,)), dma((N_SEQ,)),
            dma((GROUP,)), dma((GROUP,)),
            dma((GROUP,)), dma((GROUP,)),
            dma((N_X,)), dma((N_X,)),
            dma((N_GRP,)), dma((N_GRP,)),
            dma((N_GRP,)), dma((N_GRP,)),
            dma((N_SEQ,)), dma((N_SEQ,)),
            dma((N_X,)), dma((N_X,)),
            dma((N_Y,)), dma((N_Y,)),
            dma((N_Y,)), dma((N_Y,)),
            dma((N_X,)), dma((N_X,)),
            dma((2 * N_Y,)), dma((2 * N_Y,)),
        ],
        compiler_params=pltpu.CompilerParams(
            vmem_limit_bytes=48 * 1024 * 1024, collective_id=0, has_side_effects=True
        ),
        name="whole",
    )(frames, begins, owner[0], conv_kernel, norm_gain.reshape(1, D), w_qkv, w_out, cotangent)
    return audio.reshape(1, 128, D), grad.reshape(D, D)


def solution(mesh):
    return jax.shard_map(
        shards,
        mesh=mesh,
        in_specs=(
            P("grp", "seq", None),
            P("grp", "seq"),
            P("grp", "seq", None),
            P(),
            P(),
            P(),
            P(),
            P("grp", "seq", None),
        ),
        out_specs=(P("grp", "seq", None), P()),
        check_vma=False,
    )
```

```python
import jax
import jax.numpy as jnp
from jax import lax
from jax.experimental import pallas as pl
from jax.experimental.pallas import tpu as pltpu
from jax.sharding import PartitionSpec as P

HEADS = 8
BLOCK_LEN = 32
LEFT_BLOCKS = 2
SUB = 8
F = 512
D = 1024
LEFT = 112
RIGHT = 48
KV = 640
KOFF = 96
FAR = 1536
BIG = 1e6
F32 = jnp.float32
BF16 = jnp.bfloat16
MESH = pl.DeviceIdType.MESH
N_SEQ = 32
N_GRP = 8
N_X = 4
N_Y = 4
GROUP = 8


def bounds(bg, t0, group_len, dprev, dnext):
    lanes = FAR + F + 128
    u = lax.broadcasted_iota(jnp.int32, (1, lanes), 1) - FAR
    at = u + t0
    mark = ((bg == 1) & (at >= 0)) | (at == group_len)
    uf = u.astype(F32)
    last = jnp.where(mark, uf, -BIG)
    first = jnp.where(mark, uf, BIG)
    for c in range(KV // 128):
        window = slice(FAR - 128 + 128 * c, FAR + 128 + 128 * c)
        early = jnp.max(last[:, : FAR - 128 + 128 * c], axis=1, keepdims=True)
        t = (lax.broadcasted_iota(jnp.int32, (128, 1), 0) + (128 * c - KOFF)).astype(F32)
        before = uf[:, window] <= t
        start = jnp.max(jnp.where(before, last[:, window], -BIG), axis=1, keepdims=True)
        start = jnp.maximum(start, early)
        stop = jnp.min(jnp.where(before, BIG, first[:, window]), axis=1, keepdims=True)
        dprev[128 * c : 128 * c + 128, :] = jnp.broadcast_to(t - start, (128, 128))
        dnext[128 * c : 128 * c + 128, :] = jnp.broadcast_to(stop - t, (128, 128))


def attention_bias(dprev, dnext, bias):
    for i in range(F // 128):
        rows = slice(KOFF + 128 * i, KOFF + 128 * i + 128)
        back = dprev[rows, :].astype(jnp.int32)
        ahead = dnext[rows, :].astype(jnp.int32)
        rem = back & (BLOCK_LEN - 1)
        low = -jnp.minimum(back, rem + LEFT_BLOCKS * BLOCK_LEN)
        high = jnp.minimum(ahead, BLOCK_LEN - rem)
        for half in range(2):
            delta = (
                lax.broadcasted_iota(jnp.int32, (128, 128), 1)
                - lax.broadcasted_iota(jnp.int32, (128, 128), 0)
                + (128 * half - KOFF)
            )
            ok = (delta >= low) & (delta < high)
            bias[i, :, 128 * half : 128 * half + 128] = jnp.where(ok, F32(0.0), F32(-1e30))


def conv_norm(xf, taps, gain, dprev, dnext, hid, nrm, first, last, place_of):
    step = 32
    tiles = D // 128

    def block(n, _):
        r0, d0 = (pl.multiple_of(v, step) for v in place_of(n))
        back = dprev[pl.ds(r0, step), :]
        ahead = dnext[pl.ds(r0, step), :]
        keep = [back >= F32(4 - j) if j < 4 else ahead > F32(j - 4) for j in range(9)]
        hs = []
        total = jnp.zeros((step, 128), F32)
        for c in range(tiles):
            cols = slice(128 * c, 128 * c + 128)
            centre = xf[c, pl.ds(r0 + 16, step), :]
            acc = centre * taps[4:5, cols]
            for j in range(9):
                if j == 4:
                    continue
                term = xf[c, pl.ds(r0 + 12 + j, step), :] * taps[j : j + 1, cols]
                acc = acc + jnp.where(keep[j], term, F32(0.0))
            h16 = (centre + acc).astype(BF16)
            hid[pl.ds(r0, step), cols] = h16
            h = h16.astype(F32)
            hs.append(h)
            total = total + h
        mean = jnp.sum(total, axis=1, keepdims=True) * F32(1.0 / D)
        hs = [h - mean for h in hs]
        square = jnp.zeros((step, 128), F32)
        for h in hs:
            square = square + h * h
        var = jnp.sum(square, axis=1, keepdims=True) * F32(1.0 / D)
        scale = lax.rsqrt(var + F32(1e-5))
        for c in range(tiles):
            cols = slice(128 * c, 128 * c + 128)
            nrm[pl.ds(d0, step), cols] = (hs[c] * scale * gain[:, cols]).astype(BF16)
        return 0

    lax.fori_loop(first, last, block, 0)


def project(nrm, rows, weights, base, out, pieces):
    def tile(n, _):
        cols = pl.ds(pl.multiple_of(n * 256, 256), 256)
        value = jnp.dot(
            nrm[rows, :],
            weights[:, pl.ds(pl.multiple_of(base + n * 256, 256), 256)],
            preferred_element_type=F32,
        ).astype(BF16)
        at = 0
        for place, size in pieces:
            out[place : place + size, cols] = value[at : at + size]
            at += size
        return 0

    lax.fori_loop(0, D // 256, tile, 0)


def attend(heads, tiles, q, k, v, bias, attn):
    factor = 1.4426950408889634 / 128.0**0.5
    work = []
    for h in heads:
        lanes = pl.ds(pl.multiple_of(h * 128, 128), 128)
        for i in tiles:
            own = slice(128 * i, 128 * i + 128)
            seen = slice(128 * i, 128 * i + 256)
            s = lax.dot_general(
                q[own, lanes], k[seen, lanes], (((1,), (1,)), ((), ())), preferred_element_type=F32
            )
            work.append((own, seen, lanes, s + bias[i]))
    tops = [jnp.max(s, axis=1, keepdims=True) for _, _, _, s in work]
    expos = [jnp.exp2((item[3] - top) * factor) for item, top in zip(work, tops)]
    norms = [1.0 / jnp.sum(e, axis=1, keepdims=True) for e in expos]
    for (own, seen, lanes, _), e, norm in zip(work, expos, norms):
        w = (e * norm).astype(BF16)
        attn[own, lanes] = jnp.dot(w, v[seen, lanes], preferred_element_type=F32).astype(BF16)


def placement_of(row):
    rows = row.shape[1]
    square = lax.broadcasted_iota(jnp.int32, (rows, rows), 0) == lax.broadcasted_iota(
        jnp.int32, (rows, rows), 1
    )
    spread = jnp.where(square, row.astype(F32), F32(0.0))
    owner = jnp.sum(spread, axis=1, keepdims=True).astype(jnp.int32)
    lane = lax.broadcasted_iota(jnp.int32, (rows, 128), 1)
    hot = jnp.where(owner == lane, F32(1.0), F32(0.0))
    lower = jnp.where(
        lax.broadcasted_iota(jnp.int32, (rows, rows), 1)
        < lax.broadcasted_iota(jnp.int32, (rows, rows), 0),
        F32(1.0),
        F32(0.0),
    ).astype(BF16)
    before = jnp.dot(lower, hot.astype(BF16), preferred_element_type=F32)
    rank = jnp.sum(hot * before, axis=1, keepdims=True).astype(jnp.int32)
    slot = owner * 4 + rank
    slot_row = jnp.sum(jnp.where(square, slot.astype(F32), F32(0.0)), axis=0, keepdims=True)
    column = lax.broadcasted_iota(jnp.int32, (128, rows), 0)
    return jnp.where(column == slot_row.astype(jnp.int32), F32(1.0), F32(0.0)).astype(BF16)


def remote(src, dst, sends, recvs, index, target):
    return pltpu.make_async_remote_copy(
        src_ref=src,
        dst_ref=dst,
        send_sem=sends.at[index],
        recv_sem=recvs.at[index],
        device_id=target,
        device_id_type=MESH,
    )


def each(count, body):
    def one(k, _):
        body(k)
        return 0

    lax.fori_loop(1, count, one, 0)


def to_slots(value, wide, slots):
    for c in range(D // 128):
        wide[pl.ds(c, 128, stride=8), :] = value[:, 128 * c : 128 * c + 128].astype(F32)
    for o in range(N_SEQ):
        slots[o] = wide[32 * o : 32 * o + 32, :].astype(BF16)


def from_slots(slots, wide):
    for o in range(N_SEQ):
        wide[32 * o : 32 * o + 32, :] = slots[o].astype(F32)
    return [wide[pl.ds(c, 128, stride=8), :].astype(BF16) for c in range(D // 128)]


def whole_kernel(
    frames, begins, owner_hbm, taps_hbm, gain_hbm, wqkv_hbm, wout_hbm, cot_hbm,
    audio, fin,
    xb, xf, bgs, dprev, dnext, hid, nrm, edge, qs, ks, vs, bias, attn, wqkv, wout,
    cg, wide, place, ahl, asp, aall, perm, part, partb, xr, quarter, zr, aout, arecv,
    owner, taps, gain,
    local_sems, halo_s, halo_r, cot_s, cot_r, relay_s, relay_r, a_s, a_r, x_s, x_r, z_s, z_r,
    t_s, t_r, m_s, m_r, h0_s, h0_r, h1_s, h1_r, p0_s, p0_r, p1_s, p1_r, c_s, c_r,
):
    z = lax.axis_index("grp")
    s = lax.axis_index("seq")
    x = s // GROUP
    j = s % GROUP
    y = j // 2
    c = j % 2

    def seq(k):
        return {"seq": (s + k) % N_SEQ}

    def grp(k):
        return {"grp": (z + k) % N_GRP}

    def at_head(kx, n):
        return {"seq": (x + kx) % N_X * GROUP + (j + n) % GROUP}

    def along_x(k):
        return {"seq": (x + k) % N_X * GROUP + j}

    def along_y(k):
        return {"seq": x * GROUP + (y + k) % N_Y * 2 + c}

    other_core = {"seq": x * GROUP + y * 2 + (1 - c)}

    barrier = pltpu.get_barrier_semaphore()

    def greet(target):
        pl.semaphore_signal(barrier, inc=1, device_id=target, device_id_type=MESH)

    each(N_SEQ, lambda k: greet(seq(k)))
    each(N_GRP, lambda k: greet(grp(k)))

    def slots_of(owner_in_row):
        return pl.ds(pl.multiple_of(owner_in_row * 128, 128), 128)

    loads = [
        pltpu.make_async_copy(begins, bgs.at[3], local_sems.at[0]),
        pltpu.make_async_copy(frames.at[0], xb.at[pl.ds(LEFT, F)], local_sems.at[1]),
        pltpu.make_async_copy(taps_hbm, taps, local_sems.at[2]),
        pltpu.make_async_copy(gain_hbm, gain, local_sems.at[3]),
        pltpu.make_async_copy(cot_hbm.at[0], cg.at[slots_of(j)], local_sems.at[4]),
        pltpu.make_async_copy(owner_hbm, owner, local_sems.at[5]),
        pltpu.make_async_copy(wqkv_hbm, wqkv, local_sems.at[6]),
        pltpu.make_async_copy(wout_hbm, wout, local_sems.at[7]),
    ]
    for copy in loads:
        copy.start()
    for copy in loads[:4]:
        copy.wait()
    none = jnp.zeros((1, F), jnp.int32)
    alone = jnp.concatenate([none, none, none, bgs[3], none[:, :128]], axis=1)
    bounds(alone, s * F, F * N_SEQ, dprev, dnext)
    for tile in range(D // 128):
        xf[tile, LEFT : LEFT + F] = xb[LEFT : LEFT + F, 128 * tile : 128 * tile + 128].astype(F32)
    conv_norm(
        xf, taps, gain, dprev, dnext, hid, nrm, 0, 14, lambda n: (128 + 32 * n, 32 * n)
    )
    loads[4].wait()
    loads[5].wait()
    place[...] = placement_of(owner[...])
    loads[6].wait()
    project(nrm, slice(0, 448), wqkv, 0, qs, ((32, 448),))

    pl.semaphore_wait(barrier, N_SEQ - 1 + N_GRP - 1)

    halo = [
        remote(xb.at[pl.ds(F, LEFT)], xb.at[pl.ds(0, LEFT)], halo_s, halo_r, 0, seq(1)),
        remote(xb.at[pl.ds(LEFT, RIGHT)], xb.at[pl.ds(LEFT + F, RIGHT)], halo_s, halo_r, 1, seq(N_SEQ - 1)),
        remote(begins, bgs.at[2], halo_s, halo_r, 2, seq(1)),
        remote(begins, bgs.at[1], halo_s, halo_r, 3, seq(2)),
        remote(begins, bgs.at[0], halo_s, halo_r, 4, seq(3)),
        remote(begins, bgs.at[4], halo_s, halo_r, 5, seq(N_SEQ - 1)),
    ]
    for copy in halo:
        copy.start()

    def copy_cot(k):
        block = cg.at[slots_of(j)]
        return remote(block, block, cot_s, cot_r, k, along_y(k))

    def copy_relay(k):
        block = cg.at[slots_of((y + N_Y - k) % N_Y * 2 + c)]
        return remote(block, block, relay_s, relay_r, k, other_core)

    for k in (1, 3, 2):
        copy_cot(k).start()
    copy_relay(0).start()

    project(nrm, slice(0, 448), wqkv, D, ks, ((128, 448),))
    project(nrm, slice(0, 448), wqkv, 2 * D, vs, ((128, 448),))
    for copy in halo[2:]:
        copy.wait_recv()
    marks = jnp.concatenate([bgs[0], bgs[1], bgs[2], bgs[3], bgs[4][:, :128]], axis=1)
    bounds(marks, s * F, F * N_SEQ, dprev, dnext)
    attention_bias(dprev, dnext, bias)

    def middle(n, _):
        attend((2 * n, 2 * n + 1), (1, 2), qs, ks, vs, bias, attn)
        return 0

    lax.fori_loop(0, HEADS // 2, middle, 0)
    for copy in halo[:2]:
        copy.wait_recv()
    for tile in range(D // 128):
        cols = slice(128 * tile, 128 * tile + 128)
        xf[tile, :LEFT] = xb[:LEFT, cols].astype(F32)
        xf[tile, LEFT + F :] = xb[LEFT + F :, cols].astype(F32)
    conv_norm(
        xf, taps, gain, dprev, dnext, hid, edge, 0, 6,
        lambda n: (32 * n + 448 * (n // 4), 32 * n),
    )
    project(edge, slice(96, 160), wqkv, 0, qs, ((0, 32), (480, 32)))
    project(edge, slice(0, 192), wqkv, D, ks, ((0, 128), (576, 64)))
    project(edge, slice(0, 192), wqkv, 2 * D, vs, ((0, 128), (576, 64)))

    rows = F // SUB
    gather = jnp.where(
        lax.broadcasted_iota(jnp.int32, (rows, F), 1) >> 3
        == lax.broadcasted_iota(jnp.int32, (rows, F), 0),
        F32(1.0),
        F32(0.0),
    ).astype(BF16)

    def copy_a(kx, n):
        block = asp.at[(j + n) % HEADS, (x + kx) % N_X]
        here = pl.ds(pl.multiple_of(s * 32, 32), 32)
        return remote(block, aall.at[here], a_s, a_r, n * N_X + kx, at_head(kx, n))

    def two_heads(n, m):
        pair = ((j + n) % HEADS, (j + m) % HEADS)
        attend(pair, (0, 3), qs, ks, vs, bias, attn)
        for h in pair:
            lanes = pl.ds(pl.multiple_of(h * 128, 128), 128)
            asum = jnp.dot(gather, attn[:, lanes], preferred_element_type=F32)
            high = asum.astype(BF16)
            low = (asum - high.astype(F32)).astype(BF16)
            ahl[0, :, lanes] = high
            ahl[1, :, lanes] = low
            spread = jnp.dot(place[...], high, preferred_element_type=F32)
            spread = spread + jnp.dot(place[...], low, preferred_element_type=F32)
            for part_x in range(N_X):
                asp[h, part_x] = spread[32 * part_x : 32 * part_x + 32]

    def two_heads_and_send(p, _):
        two_heads(2 * p + 1, 2 * p + 2)
        for n in (2 * p + 1, 2 * p + 2):
            for kx in range(N_X):
                copy_a(kx, n).start()
        return 0

    lax.fori_loop(0, 3, two_heads_and_send, 0)
    two_heads(7, 0)
    for kx in range(1, N_X):
        copy_a(kx, 0).start()
    for kx in range(N_X):
        copy_a(kx, 7).start()
    aall[pl.ds(pl.multiple_of(s * 32, 32), 32), :] = asp[j, x]
    for k in (1, 3, 2):
        copy_cot(k).wait_recv()
        copy_relay(k).start()

    loads[7].wait()
    hsum = jnp.dot(gather, hid[KOFF : KOFF + F, :], preferred_element_type=F32)
    proj = jnp.dot(ahl[0], wout[...], preferred_element_type=F32)
    proj = proj + jnp.dot(ahl[1], wout[...], preferred_element_type=F32)
    pooled = ((hsum + proj) * F32(1.0 / SUB)).astype(BF16)
    dims = (((0,), (0,)), ((), ()))
    outgoing = jnp.dot(place[...], pooled, preferred_element_type=F32)
    to_slots(outgoing, wide, aout)

    def copy_audio(k):
        return remote(aout.at[(s + k) % N_SEQ], arecv.at[s], m_s, m_r, k, seq(k))

    each(N_SEQ, lambda k: copy_audio(k).start())
    arecv[s] = aout[s]

    for k in range(N_Y):
        copy_relay(k).wait_recv()

    def got_a(n, _):
        for kx in range(N_X):
            copy_a(kx, n).wait_recv()
        return 0

    for kx in range(1, N_X):
        copy_a(kx, 0).wait_recv()
    lax.fori_loop(1, HEADS, got_a, 0)
    for m in range(GROUP):
        for rank in range(4):
            perm[pl.ds(m * 128 + rank, N_SEQ, stride=4), :] = aall[
                pl.ds(m * 4 + rank, N_SEQ, stride=32), :
            ]
    apart = perm[...]
    ahigh = apart.astype(BF16)
    alow = (apart - ahigh.astype(F32)).astype(BF16)
    part[...] = lax.dot_general(ahigh, cg[...], dims, preferred_element_type=F32)
    part[...] += lax.dot_general(alow, cg[...], dims, preferred_element_type=F32)
    partb[...] = part[...].astype(BF16)

    def rows_of(place_x):
        return pl.ds(pl.multiple_of(place_x * 32, 32), 32)

    def copy_x(k):
        return remote(partb.at[rows_of((x + k) % N_X)], xr.at[k], x_s, x_r, k, along_x(k))

    for k in range(1, N_X):
        copy_x(k).start()
    for k in range(1, N_X):
        copy_x(k).wait_recv()
    total = part[rows_of(x), :]
    for k in range(1, N_X):
        total = total + xr[k].astype(F32)
    for tile in range(N_GRP):
        quarter[tile] = total[:, 128 * tile : 128 * tile + 128]

    def copy_z(k):
        return remote(quarter.at[(z + k) % N_GRP], zr.at[k], z_s, z_r, k, grp(k))

    for k in range(1, N_GRP):
        copy_z(k).start()
    for k in range(1, N_GRP):
        copy_z(k).wait_recv()
    tile_sum = quarter[z]
    for k in range(1, N_GRP):
        tile_sum = tile_sum + zr[k]
    own_cols = pl.ds(pl.multiple_of(z * 128, 128), 128)
    fin[y, c, x, :, own_cols] = (tile_sum * F32(1.0 / (128 * SUB))).astype(BF16)

    def copy_t(k):
        tile = fin.at[y, c, x, :, own_cols]
        return remote(tile, tile, t_s, t_r, k, grp(k))

    for k in range(1, N_GRP):
        copy_t(k).start()
    for k in range(1, N_GRP):
        copy_t(k).wait_recv()

    first, second = pl.ds(0, D // 2), pl.ds(D // 2, D // 2)

    def copy_h0(k):
        block = fin.at[y, c, x, :, first]
        return remote(block, block, h0_s, h0_r, k, along_x(k))

    def copy_h1(k):
        block = fin.at[y, c, x, :, second]
        return remote(block, block, h1_s, h1_r, k, along_y(k))

    def copy_p0(kx, ky):
        block = fin.at[y, c, (x + N_X - kx) % N_X, :, first]
        return remote(block, block, p0_s, p0_r, kx * N_Y + ky, along_y(ky))

    def copy_p1(ky, kx):
        block = fin.at[(y + N_Y - ky) % N_Y, c, x, :, second]
        return remote(block, block, p1_s, p1_r, ky * N_X + kx, along_x(kx))

    def copy_c0(k):
        block = fin.at[(y + N_Y - k) % N_Y, c, :, :, first]
        return remote(block, block, c_s, c_r, k, other_core)

    def copy_c1(k):
        block = fin.at[:, c, (x + N_X - k) % N_X, :, second]
        return remote(block, block, c_s, c_r, N_Y + k, other_core)

    for k in (1, 3, 2):
        copy_h0(k).start()
        copy_h1(k).start()
    for k in (1, 3, 2):
        copy_p0(0, k).start()
        copy_p1(0, k).start()
    for k in (1, 3, 2):
        copy_h0(k).wait_recv()
        for ky in (1, 3, 2):
            copy_p0(k, ky).start()
        copy_h1(k).wait_recv()
        for kx in (1, 3, 2):
            copy_p1(k, kx).start()
    copy_c0(0).start()
    copy_c1(0).start()

    def got_audio(k):
        source = (s + N_SEQ - k) % N_SEQ
        remote(arecv.at[source], arecv.at[source], m_s, m_r, k, seq(k)).wait_recv()

    each(N_SEQ, got_audio)
    for tile, value in enumerate(from_slots(arecv, wide)):
        audio[:, 128 * tile : 128 * tile + 128] = value

    for k in (1, 3, 2):
        for other in range(N_X):
            copy_p0(other, k).wait_recv()
        copy_c0(k).start()
        for other in range(N_Y):
            copy_p1(other, k).wait_recv()
        copy_c1(k).start()
    for k in range(N_Y):
        copy_c0(k).wait_recv()
        copy_c1(k).wait_recv()

    for copy in halo:
        copy.wait_send()

    each(N_SEQ, lambda k: copy_audio(k).wait_send())

    def sent_a(n, _):
        for kx in range(N_X):
            copy_a(kx, n).wait_send()
        return 0

    for kx in range(1, N_X):
        copy_a(kx, 0).wait_send()
    lax.fori_loop(1, HEADS, sent_a, 0)

    def sent_z(k):
        copy_z(k).wait_send()
        copy_t(k).wait_send()

    each(N_GRP, sent_z)
    for k in range(1, N_X):
        copy_cot(k).wait_send()
        copy_x(k).wait_send()
        copy_h0(k).wait_send()
        copy_h1(k).wait_send()
    for k in range(N_Y):
        copy_relay(k).wait_send()
        copy_c0(k).wait_send()
        copy_c1(k).wait_send()
        for other in range(1, N_X):
            copy_p0(k, other).wait_send()
            copy_p1(k, other).wait_send()


def shards(frames, begins, owner, conv_kernel, norm_gain, w_qkv, w_out, cotangent):
    vm = pl.BlockSpec(memory_space=pltpu.VMEM)
    hbm = pl.BlockSpec(memory_space=pltpu.HBM)
    dma = pltpu.SemaphoreType.DMA
    audio, grad = pl.pallas_call(
        whole_kernel,
        out_shape=(
            jax.ShapeDtypeStruct((128, D), BF16),
            jax.ShapeDtypeStruct((N_Y, 2, N_X, 32, D), BF16),
        ),
        in_specs=[hbm] * 8,
        out_specs=(vm, vm),
        scratch_shapes=[
            pltpu.VMEM((LEFT + F + RIGHT, D), BF16),
            pltpu.VMEM((8, LEFT + F + RIGHT, 128), F32),
            pltpu.VMEM((5, 1, F), jnp.int32),
            pltpu.VMEM((KV, 128), F32),
            pltpu.VMEM((KV, 128), F32),
            pltpu.VMEM((KV, D), BF16),
            pltpu.VMEM((448, D), BF16),
            pltpu.VMEM((192, D), BF16),
            pltpu.VMEM((F, D), BF16),
            pltpu.VMEM((KV, D), BF16),
            pltpu.VMEM((KV, D), BF16),
            pltpu.VMEM((4, 128, 256), F32),
            pltpu.VMEM((F, D), BF16),
            pltpu.VMEM((D, 3 * D), BF16),
            pltpu.VMEM((D, D), BF16),
            pltpu.VMEM((GROUP * 128, D), BF16),
            pltpu.VMEM((1024, 128), F32),
            pltpu.VMEM((128, 64), BF16),
            pltpu.VMEM((2, 64, D), BF16),
            pltpu.VMEM((HEADS, N_X, 32, 128), F32),
            pltpu.VMEM((1024, 128), F32),
            pltpu.VMEM((1024, 128), F32),
            pltpu.VMEM((128, D), F32),
            pltpu.VMEM((128, D), BF16),
            pltpu.VMEM((N_X, 32, D), BF16),
            pltpu.VMEM((N_GRP, 32, 128), F32),
            pltpu.VMEM((N_GRP, 32, 128), F32),
            pltpu.VMEM((N_SEQ, 32, 128), BF16),
            pltpu.VMEM((N_SEQ, 32, 128), BF16),
            pltpu.VMEM((1, 64), jnp.int32),
            pltpu.VMEM((9, D), F32),
            pltpu.VMEM((1, D), F32),
            dma((8,)),
            dma((6,)), dma((6,)),
            dma((N_Y,)), dma((N_Y,)),
            dma((N_Y,)), dma((N_Y,)),
            dma((N_SEQ,)), dma((N_SEQ,)),
            dma((N_X,)), dma((N_X,)),
            dma((N_GRP,)), dma((N_GRP,)),
            dma((N_GRP,)), dma((N_GRP,)),
            dma((N_SEQ,)), dma((N_SEQ,)),
            dma((N_X,)), dma((N_X,)),
            dma((N_Y,)), dma((N_Y,)),
            dma((N_X * N_Y,)), dma((N_X * N_Y,)),
            dma((N_X * N_Y,)), dma((N_X * N_Y,)),
            dma((2 * N_Y,)), dma((2 * N_Y,)),
        ],
        compiler_params=pltpu.CompilerParams(
            vmem_limit_bytes=48 * 1024 * 1024, collective_id=0, has_side_effects=True
        ),
        name="whole",
    )(
        *(
            pltpu.with_memory_space_constraint(value, pltpu.HBM)
            for value in (
                frames,
                begins,
                owner.reshape(1, 64),
                conv_kernel,
                norm_gain.reshape(1, D),
                w_qkv,
                w_out,
                cotangent,
            )
        )
    )
    return audio.reshape(1, 128, D), grad.reshape(D, D)


def solution(mesh):
    return jax.shard_map(
        shards,
        mesh=mesh,
        in_specs=(
            P("grp", "seq", None),
            P("grp", "seq"),
            P("grp", "seq", None),
            P(),
            P(),
            P(),
            P(),
            P("grp", "seq", None),
        ),
        out_specs=(P("grp", "seq", None), P()),
        check_vma=False,
    )
```

```python
import jax
import jax.numpy as jnp
from jax import lax
from jax.experimental import pallas as pl
from jax.experimental.pallas import tpu as pltpu
from jax.sharding import PartitionSpec as P

HEADS = 8
BLOCK_LEN = 32
LEFT_BLOCKS = 2
SUB = 8
F = 512
D = 1024
LEFT = 112
RIGHT = 48
KV = 640
KOFF = 96
FAR = 1536
BIG = 1e6
F32 = jnp.float32
BF16 = jnp.bfloat16
MESH = pl.DeviceIdType.MESH
N_SEQ = 32
N_GRP = 8
N_X = 4
N_Y = 4
GROUP = 8


def bounds(bg, t0, group_len, dprev, dnext):
    lanes = FAR + F + 128
    u = lax.broadcasted_iota(jnp.int32, (1, lanes), 1) - FAR
    at = u + t0
    mark = ((bg == 1) & (at >= 0)) | (at == group_len)
    uf = u.astype(F32)
    last = jnp.where(mark, uf, -BIG)
    first = jnp.where(mark, uf, BIG)
    for c in range(KV // 128):
        window = slice(FAR - 128 + 128 * c, FAR + 128 + 128 * c)
        early = jnp.max(last[:, : FAR - 128 + 128 * c], axis=1, keepdims=True)
        t = (lax.broadcasted_iota(jnp.int32, (128, 1), 0) + (128 * c - KOFF)).astype(F32)
        before = uf[:, window] <= t
        start = jnp.max(jnp.where(before, last[:, window], -BIG), axis=1, keepdims=True)
        start = jnp.maximum(start, early)
        stop = jnp.min(jnp.where(before, BIG, first[:, window]), axis=1, keepdims=True)
        dprev[128 * c : 128 * c + 128, :] = jnp.broadcast_to(t - start, (128, 128))
        dnext[128 * c : 128 * c + 128, :] = jnp.broadcast_to(stop - t, (128, 128))


def attention_bias(dprev, dnext, bias):
    for i in range(F // 128):
        rows = slice(KOFF + 128 * i, KOFF + 128 * i + 128)
        back = dprev[rows, :].astype(jnp.int32)
        ahead = dnext[rows, :].astype(jnp.int32)
        rem = back & (BLOCK_LEN - 1)
        low = -jnp.minimum(back, rem + LEFT_BLOCKS * BLOCK_LEN)
        high = jnp.minimum(ahead, BLOCK_LEN - rem)
        for half in range(2):
            delta = (
                lax.broadcasted_iota(jnp.int32, (128, 128), 1)
                - lax.broadcasted_iota(jnp.int32, (128, 128), 0)
                + (128 * half - KOFF)
            )
            ok = (delta >= low) & (delta < high)
            bias[i, :, 128 * half : 128 * half + 128] = jnp.where(ok, F32(0.0), F32(-1e30))


def conv_norm(xf, taps, gain, dprev, dnext, hid, nrm, first, last, place_of):
    step = 32
    tiles = D // 128

    def block(n, _):
        r0, d0 = (pl.multiple_of(v, step) for v in place_of(n))
        back = dprev[pl.ds(r0, step), :]
        ahead = dnext[pl.ds(r0, step), :]
        keep = [back >= F32(4 - j) if j < 4 else ahead > F32(j - 4) for j in range(9)]
        hs = []
        total = jnp.zeros((step, 128), F32)
        for c in range(tiles):
            cols = slice(128 * c, 128 * c + 128)
            centre = xf[c, pl.ds(r0 + 16, step), :]
            acc = centre * taps[4:5, cols]
            for j in range(9):
                if j == 4:
                    continue
                term = xf[c, pl.ds(r0 + 12 + j, step), :] * taps[j : j + 1, cols]
                acc = acc + jnp.where(keep[j], term, F32(0.0))
            h16 = (centre + acc).astype(BF16)
            hid[pl.ds(r0, step), cols] = h16
            h = h16.astype(F32)
            hs.append(h)
            total = total + h
        mean = jnp.sum(total, axis=1, keepdims=True) * F32(1.0 / D)
        hs = [h - mean for h in hs]
        square = jnp.zeros((step, 128), F32)
        for h in hs:
            square = square + h * h
        var = jnp.sum(square, axis=1, keepdims=True) * F32(1.0 / D)
        scale = lax.rsqrt(var + F32(1e-5))
        for c in range(tiles):
            cols = slice(128 * c, 128 * c + 128)
            nrm[pl.ds(d0, step), cols] = (hs[c] * scale * gain[:, cols]).astype(BF16)
        return 0

    lax.fori_loop(first, last, block, 0)


def project(nrm, rows, weights, base, out, pieces):
    value = jnp.dot(
        nrm[rows, :], weights[:, base : base + D], preferred_element_type=F32
    ).astype(BF16)
    at = 0
    for place, size in pieces:
        out[place : place + size, :] = value[at : at + size]
        at += size


def attend(heads, tiles, q, k, v, bias, attn):
    factor = 1.4426950408889634 / 128.0**0.5
    work = []
    for h in heads:
        lanes = pl.ds(pl.multiple_of(h * 128, 128), 128)
        for i in tiles:
            own = slice(128 * i, 128 * i + 128)
            seen = slice(128 * i, 128 * i + 256)
            s = lax.dot_general(
                q[own, lanes], k[seen, lanes], (((1,), (1,)), ((), ())), preferred_element_type=F32
            )
            work.append((own, seen, lanes, s + bias[i]))
    tops = [jnp.max(s, axis=1, keepdims=True) for _, _, _, s in work]
    expos = [jnp.exp2((item[3] - top) * factor) for item, top in zip(work, tops)]
    norms = [1.0 / jnp.sum(e, axis=1, keepdims=True) for e in expos]
    for (own, seen, lanes, _), e, norm in zip(work, expos, norms):
        w = (e * norm).astype(BF16)
        attn[own, lanes] = jnp.dot(w, v[seen, lanes], preferred_element_type=F32).astype(BF16)


def placement_of(row):
    rows = row.shape[1]
    square = lax.broadcasted_iota(jnp.int32, (rows, rows), 0) == lax.broadcasted_iota(
        jnp.int32, (rows, rows), 1
    )
    spread = jnp.where(square, row.astype(F32), F32(0.0))
    owner = jnp.sum(spread, axis=1, keepdims=True).astype(jnp.int32)
    lane = lax.broadcasted_iota(jnp.int32, (rows, 128), 1)
    hot = jnp.where(owner == lane, F32(1.0), F32(0.0))
    lower = jnp.where(
        lax.broadcasted_iota(jnp.int32, (rows, rows), 1)
        < lax.broadcasted_iota(jnp.int32, (rows, rows), 0),
        F32(1.0),
        F32(0.0),
    ).astype(BF16)
    before = jnp.dot(lower, hot.astype(BF16), preferred_element_type=F32)
    rank = jnp.sum(hot * before, axis=1, keepdims=True).astype(jnp.int32)
    slot = owner * 4 + rank
    slot_row = jnp.sum(jnp.where(square, slot.astype(F32), F32(0.0)), axis=0, keepdims=True)
    column = lax.broadcasted_iota(jnp.int32, (128, rows), 0)
    by_slot = jnp.where(column == slot_row.astype(jnp.int32), F32(1.0), F32(0.0)).astype(BF16)
    by_row = jnp.where(lane == slot, F32(1.0), F32(0.0)).astype(BF16)
    return by_slot, by_row


def remote(src, dst, sends, recvs, index, target):
    return pltpu.make_async_remote_copy(
        src_ref=src,
        dst_ref=dst,
        send_sem=sends.at[index],
        recv_sem=recvs.at[index],
        device_id=target,
        device_id_type=MESH,
    )


def each(count, body):
    def one(k, _):
        body(k)
        return 0

    lax.fori_loop(1, count, one, 0)


def to_slots(value, wide, slots):
    for c in range(D // 128):
        wide[pl.ds(c, 128, stride=8), :] = value[:, 128 * c : 128 * c + 128].astype(F32)
    for o in range(N_SEQ):
        slots[o] = wide[32 * o : 32 * o + 32, :].astype(BF16)


def from_slots(slots, wide):
    for o in range(N_SEQ):
        wide[32 * o : 32 * o + 32, :] = slots[o].astype(F32)
    return [wide[pl.ds(c, 128, stride=8), :].astype(BF16) for c in range(D // 128)]


def whole_kernel(
    frames, begins, owner_hbm, taps_hbm, gain_hbm, wqkv_hbm, wout_hbm, cot_hbm,
    audio, fin,
    xb, xf, bgs, dprev, dnext, hid, nrm, edge, qs, ks, vs, bias, attn, wqkv, wout,
    cotv, cots, back, gall, wide, place, pick, ahl, asp, aall, part, tiles, got, aout, arecv,
    owner, taps, gain,
    local_sems, halo_s, halo_r, cot_s, cot_r, g_s, g_r, relay_s, relay_r, a_s, a_r, xz_s, xz_r,
    t_s, t_r, m_s, m_r, h0_s, h0_r, h1_s, h1_r, p0_s, p0_r, p1_s, p1_r, c_s, c_r,
):
    z = lax.axis_index("grp")
    s = lax.axis_index("seq")
    x = s // GROUP
    j = s % GROUP
    y = j // 2
    c = j % 2

    def seq(k):
        return {"seq": (s + k) % N_SEQ}

    def grp(k):
        return {"grp": (z + k) % N_GRP}

    def in_group(k):
        return {"seq": x * GROUP + (j + k) % GROUP}

    def along_x(k):
        return {"seq": (x + k) % N_X * GROUP + j}

    def along_y(k):
        return {"seq": x * GROUP + (y + k) % N_Y * 2 + c}

    other_core = {"seq": x * GROUP + y * 2 + (1 - c)}

    barrier = pltpu.get_barrier_semaphore()

    def greet(target):
        pl.semaphore_signal(barrier, inc=1, device_id=target, device_id_type=MESH)

    def across(k):
        return {"grp": (z + k % N_GRP) % N_GRP, "seq": (x + k // N_GRP) % N_X * GROUP + j}

    each(N_SEQ, lambda k: greet(seq(k)))

    def greet_planes(kz):
        for kx in range(N_X):
            greet(across(kx * N_GRP + kz))

    each(N_GRP, greet_planes)

    def rows_of(source):
        return pl.ds(pl.multiple_of(source * 64, 64), 64)

    loads = [
        pltpu.make_async_copy(begins, bgs.at[3], local_sems.at[0]),
        pltpu.make_async_copy(frames.at[0], xb.at[pl.ds(LEFT, F)], local_sems.at[1]),
        pltpu.make_async_copy(taps_hbm, taps, local_sems.at[2]),
        pltpu.make_async_copy(gain_hbm, gain, local_sems.at[3]),
        pltpu.make_async_copy(cot_hbm.at[0], cotv, local_sems.at[4]),
        pltpu.make_async_copy(owner_hbm, owner, local_sems.at[5]),
        pltpu.make_async_copy(wqkv_hbm, wqkv, local_sems.at[6]),
        pltpu.make_async_copy(wout_hbm, wout, local_sems.at[7]),
    ]
    for copy in loads:
        copy.start()
    pl.semaphore_wait(barrier, N_SEQ - 1 + N_X * (N_GRP - 1))

    halo = [
        remote(frames.at[0, pl.ds(F - LEFT, LEFT)], xb.at[pl.ds(0, LEFT)], halo_s, halo_r, 0, seq(1)),
        remote(frames.at[0, pl.ds(0, RIGHT)], xb.at[pl.ds(LEFT + F, RIGHT)], halo_s, halo_r, 1, seq(N_SEQ - 1)),
        remote(begins, bgs.at[2], halo_s, halo_r, 2, seq(1)),
        remote(begins, bgs.at[1], halo_s, halo_r, 3, seq(2)),
        remote(begins, bgs.at[0], halo_s, halo_r, 4, seq(3)),
        remote(begins, bgs.at[4], halo_s, halo_r, 5, seq(N_SEQ - 1)),
    ]
    for copy in halo[2:] + halo[:2]:
        copy.start()

    loads[4].wait()
    to_slots(cotv[...], wide, cots)

    def copy_cot(k):
        return remote(cots.at[(s + k) % N_SEQ], back.at[s], cot_s, cot_r, k, seq(k))

    each(N_SEQ, lambda k: copy_cot(k).start())
    back[s] = cots[s]

    for copy in loads[:4]:
        copy.wait()
    none = jnp.zeros((1, F), jnp.int32)
    alone = jnp.concatenate([none, none, none, bgs[3], none[:, :128]], axis=1)
    bounds(alone, s * F, F * N_SEQ, dprev, dnext)
    for tile in range(D // 128):
        xf[tile, LEFT : LEFT + F] = xb[LEFT : LEFT + F, 128 * tile : 128 * tile + 128].astype(F32)
    conv_norm(
        xf, taps, gain, dprev, dnext, hid, nrm, 0, 14, lambda n: (128 + 32 * n, 32 * n)
    )
    loads[5].wait()
    place[...], pick[...] = placement_of(owner[...])
    loads[6].wait()
    project(nrm, slice(0, 448), wqkv, 0, qs, ((32, 448),))

    project(nrm, slice(0, 448), wqkv, D, ks, ((128, 448),))
    project(nrm, slice(0, 448), wqkv, 2 * D, vs, ((128, 448),))
    for copy in halo[2:]:
        copy.wait_recv()
    marks = jnp.concatenate([bgs[0], bgs[1], bgs[2], bgs[3], bgs[4][:, :128]], axis=1)
    bounds(marks, s * F, F * N_SEQ, dprev, dnext)
    attention_bias(dprev, dnext, bias)

    def middle(n, _):
        attend((2 * n, 2 * n + 1), (1, 2), qs, ks, vs, bias, attn)
        return 0

    lax.fori_loop(0, HEADS // 2, middle, 0)

    def got_cot(k):
        source = (s + N_SEQ - k) % N_SEQ
        remote(back.at[source], back.at[source], cot_s, cot_r, k, seq(k)).wait_recv()

    each(N_SEQ, got_cot)
    for tile, value in enumerate(from_slots(back, wide)):
        gall[rows_of(j), 128 * tile : 128 * tile + 128] = jnp.dot(
            pick[...], value, preferred_element_type=F32
        ).astype(BF16)

    def copy_g(k):
        block = gall.at[rows_of(j)]
        return remote(block, block, g_s, g_r, k, along_y(k))

    def copy_relay(k):
        block = gall.at[rows_of((y + N_Y - k) % N_Y * 2 + c)]
        return remote(block, block, relay_s, relay_r, k, other_core)

    for k in (1, 3, 2):
        copy_g(k).start()
    copy_relay(0).start()
    for copy in halo[:2]:
        copy.wait_recv()
    for tile in range(D // 128):
        cols = slice(128 * tile, 128 * tile + 128)
        xf[tile, :LEFT] = xb[:LEFT, cols].astype(F32)
        xf[tile, LEFT + F :] = xb[LEFT + F :, cols].astype(F32)
    conv_norm(
        xf, taps, gain, dprev, dnext, hid, edge, 0, 6,
        lambda n: (32 * n + 448 * (n // 4), 32 * n),
    )
    project(edge, slice(96, 160), wqkv, 0, qs, ((0, 32), (480, 32)))
    project(edge, slice(0, 192), wqkv, D, ks, ((0, 128), (576, 64)))
    project(edge, slice(0, 192), wqkv, 2 * D, vs, ((0, 128), (576, 64)))

    rows = F // SUB
    gather = jnp.where(
        lax.broadcasted_iota(jnp.int32, (rows, F), 1) >> 3
        == lax.broadcasted_iota(jnp.int32, (rows, F), 0),
        F32(1.0),
        F32(0.0),
    ).astype(BF16)

    def copy_a(n):
        return remote(asp.at[(j + n) % HEADS], aall.at[:, rows_of(j)], a_s, a_r, n, in_group(n))

    def two_heads(n, m):
        pair = ((j + n) % HEADS, (j + m) % HEADS)
        attend(pair, (0, 3), qs, ks, vs, bias, attn)
        for h in pair:
            lanes = pl.ds(pl.multiple_of(h * 128, 128), 128)
            asum = jnp.dot(gather, attn[:, lanes], preferred_element_type=F32)
            high = asum.astype(BF16)
            low = (asum - high.astype(F32)).astype(BF16)
            ahl[0, :, lanes] = high
            ahl[1, :, lanes] = low
            asp[h, 0] = high
            asp[h, 1] = low

    def two_heads_and_send(p, _):
        two_heads(2 * p + 1, 2 * p + 2)
        copy_a(2 * p + 1).start()
        copy_a(2 * p + 2).start()
        return 0

    lax.fori_loop(0, 3, two_heads_and_send, 0)
    two_heads(7, 0)
    copy_a(7).start()
    aall[:, rows_of(j), :] = asp[j]
    for k in (1, 3, 2):
        copy_g(k).wait_recv()
        copy_relay(k).start()

    loads[7].wait()
    hsum = jnp.dot(gather, hid[KOFF : KOFF + F, :], preferred_element_type=F32)
    proj = jnp.dot(ahl[0], wout[...], preferred_element_type=F32)
    proj = proj + jnp.dot(ahl[1], wout[...], preferred_element_type=F32)
    pooled = ((hsum + proj) * F32(1.0 / SUB)).astype(BF16)
    dims = (((0,), (0,)), ((), ()))
    outgoing = jnp.dot(place[...], pooled, preferred_element_type=F32)
    to_slots(outgoing, wide, aout)

    def copy_audio(k):
        return remote(aout.at[(s + k) % N_SEQ], arecv.at[s], m_s, m_r, k, seq(k))

    each(N_SEQ, lambda k: copy_audio(k).start())
    arecv[s] = aout[s]

    for k in range(N_Y):
        copy_relay(k).wait_recv()

    each(GROUP, lambda k: copy_a(k).wait_recv())
    part[...] = lax.dot_general(aall[0], gall[...], dims, preferred_element_type=F32)
    part[...] += lax.dot_general(aall[1], gall[...], dims, preferred_element_type=F32)
    for px in range(N_X):
        for pz in range(N_GRP):
            tiles[px, pz] = part[32 * px : 32 * px + 32, 128 * pz : 128 * pz + 128].astype(BF16)

    def copy_xz(k):
        block = tiles.at[(x + k // N_GRP) % N_X, (z + k % N_GRP) % N_GRP]
        return remote(block, got.at[k], xz_s, xz_r, k, across(k))

    each(N_X * N_GRP, lambda k: copy_xz(k).start())
    tile_sum = part[
        pl.ds(pl.multiple_of(x * 32, 32), 32), pl.ds(pl.multiple_of(z * 128, 128), 128)
    ]
    each(N_X * N_GRP, lambda k: copy_xz(k).wait_recv())
    for k in range(1, N_X * N_GRP):
        tile_sum = tile_sum + got[k].astype(F32)
    own_cols = pl.ds(pl.multiple_of(z * 128, 128), 128)
    fin[y, c, x, :, own_cols] = (tile_sum * F32(1.0 / (128 * SUB))).astype(BF16)

    def copy_t(k):
        tile = fin.at[y, c, x, :, own_cols]
        return remote(tile, tile, t_s, t_r, k, grp(k))

    for k in range(1, N_GRP):
        copy_t(k).start()
    for k in range(1, N_GRP):
        copy_t(k).wait_recv()

    first, second = pl.ds(0, D // 2), pl.ds(D // 2, D // 2)

    def copy_h0(k):
        block = fin.at[y, c, x, :, first]
        return remote(block, block, h0_s, h0_r, k, along_x(k))

    def copy_h1(k):
        block = fin.at[y, c, x, :, second]
        return remote(block, block, h1_s, h1_r, k, along_y(k))

    def copy_p0(kx, ky):
        block = fin.at[y, c, (x + N_X - kx) % N_X, :, first]
        return remote(block, block, p0_s, p0_r, kx * N_Y + ky, along_y(ky))

    def copy_p1(ky, kx):
        block = fin.at[(y + N_Y - ky) % N_Y, c, x, :, second]
        return remote(block, block, p1_s, p1_r, ky * N_X + kx, along_x(kx))

    def copy_c0(k):
        block = fin.at[(y + N_Y - k) % N_Y, c, :, :, first]
        return remote(block, block, c_s, c_r, k, other_core)

    def copy_c1(k):
        block = fin.at[:, c, (x + N_X - k) % N_X, :, second]
        return remote(block, block, c_s, c_r, N_Y + k, other_core)

    for k in (1, 3, 2):
        copy_h0(k).start()
        copy_h1(k).start()
    for k in (1, 3, 2):
        copy_p0(0, k).start()
        copy_p1(0, k).start()
    for k in (1, 3, 2):
        copy_h0(k).wait_recv()
        for ky in (1, 3, 2):
            copy_p0(k, ky).start()
        copy_h1(k).wait_recv()
        for kx in (1, 3, 2):
            copy_p1(k, kx).start()
    copy_c0(0).start()
    copy_c1(0).start()

    def got_audio(k):
        source = (s + N_SEQ - k) % N_SEQ
        remote(arecv.at[source], arecv.at[source], m_s, m_r, k, seq(k)).wait_recv()

    each(N_SEQ, got_audio)
    for tile, value in enumerate(from_slots(arecv, wide)):
        audio[:, 128 * tile : 128 * tile + 128] = value

    for k in (1, 3, 2):
        for other in range(N_X):
            copy_p0(other, k).wait_recv()
        copy_c0(k).start()
        for other in range(N_Y):
            copy_p1(other, k).wait_recv()
        copy_c1(k).start()
    for k in range(N_Y):
        copy_c0(k).wait_recv()
        copy_c1(k).wait_recv()

    for copy in halo:
        copy.wait_send()

    each(N_SEQ, lambda k: copy_audio(k).wait_send())

    each(N_SEQ, lambda k: copy_cot(k).wait_send())
    each(GROUP, lambda k: copy_a(k).wait_send())
    each(N_X * N_GRP, lambda k: copy_xz(k).wait_send())
    each(N_GRP, lambda k: copy_t(k).wait_send())
    for k in range(1, N_X):
        copy_g(k).wait_send()
        copy_h0(k).wait_send()
        copy_h1(k).wait_send()
    for k in range(N_Y):
        copy_relay(k).wait_send()
        copy_c0(k).wait_send()
        copy_c1(k).wait_send()
        for other in range(1, N_X):
            copy_p0(k, other).wait_send()
            copy_p1(k, other).wait_send()


def shards(frames, begins, owner, conv_kernel, norm_gain, w_qkv, w_out, cotangent):
    vm = pl.BlockSpec(memory_space=pltpu.VMEM)
    hbm = pl.BlockSpec(memory_space=pltpu.HBM)
    dma = pltpu.SemaphoreType.DMA
    audio, grad = pl.pallas_call(
        whole_kernel,
        out_shape=(
            jax.ShapeDtypeStruct((128, D), BF16),
            jax.ShapeDtypeStruct((N_Y, 2, N_X, 32, D), BF16),
        ),
        in_specs=[hbm] * 8,
        out_specs=(vm, vm),
        scratch_shapes=[
            pltpu.VMEM((LEFT + F + RIGHT, D), BF16),
            pltpu.VMEM((8, LEFT + F + RIGHT, 128), F32),
            pltpu.VMEM((5, 1, F), jnp.int32),
            pltpu.VMEM((KV, 128), F32),
            pltpu.VMEM((KV, 128), F32),
            pltpu.VMEM((KV, D), BF16),
            pltpu.VMEM((448, D), BF16),
            pltpu.VMEM((192, D), BF16),
            pltpu.VMEM((F, D), BF16),
            pltpu.VMEM((KV, D), BF16),
            pltpu.VMEM((KV, D), BF16),
            pltpu.VMEM((4, 128, 256), F32),
            pltpu.VMEM((F, D), BF16),
            pltpu.VMEM((D, 3 * D), BF16),
            pltpu.VMEM((D, D), BF16),
            pltpu.VMEM((128, D), BF16),
            pltpu.VMEM((N_SEQ, 32, 128), BF16),
            pltpu.VMEM((N_SEQ, 32, 128), BF16),
            pltpu.VMEM((GROUP * 64, D), BF16),
            pltpu.VMEM((1024, 128), F32),
            pltpu.VMEM((128, 64), BF16),
            pltpu.VMEM((64, 128), BF16),
            pltpu.VMEM((2, 64, D), BF16),
            pltpu.VMEM((HEADS, 2, 64, 128), BF16),
            pltpu.VMEM((2, GROUP * 64, 128), BF16),
            pltpu.VMEM((128, D), F32),
            pltpu.VMEM((N_X, N_GRP, 32, 128), BF16),
            pltpu.VMEM((N_X * N_GRP, 32, 128), BF16),
            pltpu.VMEM((N_SEQ, 32, 128), BF16),
            pltpu.VMEM((N_SEQ, 32, 128), BF16),
            pltpu.VMEM((1, 64), jnp.int32),
            pltpu.VMEM((9, D), F32),
            pltpu.VMEM((1, D), F32),
            dma((8,)),
            dma((6,)), dma((6,)),
            dma((N_SEQ,)), dma((N_SEQ,)),
            dma((N_Y,)), dma((N_Y,)),
            dma((N_Y,)), dma((N_Y,)),
            dma((GROUP,)), dma((GROUP,)),
            dma((N_X * N_GRP,)), dma((N_X * N_GRP,)),
            dma((N_GRP,)), dma((N_GRP,)),
            dma((N_SEQ,)), dma((N_SEQ,)),
            dma((N_X,)), dma((N_X,)),
            dma((N_Y,)), dma((N_Y,)),
            dma((N_X * N_Y,)), dma((N_X * N_Y,)),
            dma((N_X * N_Y,)), dma((N_X * N_Y,)),
            dma((2 * N_Y,)), dma((2 * N_Y,)),
        ],
        compiler_params=pltpu.CompilerParams(
            vmem_limit_bytes=48 * 1024 * 1024, collective_id=0, has_side_effects=True
        ),
        name="whole",
    )(
        *(
            pltpu.with_memory_space_constraint(value, pltpu.HBM)
            for value in (
                frames,
                begins,
                owner.reshape(1, 64),
                conv_kernel,
                norm_gain.reshape(1, D),
                w_qkv,
                w_out,
                cotangent,
            )
        )
    )
    return audio.reshape(1, 128, D), grad.reshape(D, D)


def solution(mesh):
    return jax.shard_map(
        shards,
        mesh=mesh,
        in_specs=(
            P("grp", "seq", None),
            P("grp", "seq"),
            P("grp", "seq", None),
            P(),
            P(),
            P(),
            P(),
            P("grp", "seq", None),
        ),
        out_specs=(P("grp", "seq", None), P()),
        check_vma=False,
    )
```

```python
import jax
import jax.numpy as jnp
from jax import lax
from jax.experimental import pallas as pl
from jax.experimental.pallas import tpu as pltpu
from jax.sharding import PartitionSpec as P

HEADS = 8
BLOCK_LEN = 32
LEFT_BLOCKS = 2
SUB = 8
F = 512
D = 1024
LEFT = 112
RIGHT = 48
KV = 640
KOFF = 96
FAR = 1536
BIG = 1e6
F32 = jnp.float32
BF16 = jnp.bfloat16
MESH = pl.DeviceIdType.MESH
N_SEQ = 32
N_GRP = 8
N_X = 4
N_Y = 4
GROUP = 8


def bounds(bg, t0, group_len, dprev, dnext):
    lanes = FAR + F + 128
    u = lax.broadcasted_iota(jnp.int32, (1, lanes), 1) - FAR
    at = u + t0
    mark = ((bg == 1) & (at >= 0)) | (at == group_len)
    uf = u.astype(F32)
    last = jnp.where(mark, uf, -BIG)
    first = jnp.where(mark, uf, BIG)
    for c in range(KV // 128):
        window = slice(FAR - 128 + 128 * c, FAR + 128 + 128 * c)
        early = jnp.max(last[:, : FAR - 128 + 128 * c], axis=1, keepdims=True)
        t = (lax.broadcasted_iota(jnp.int32, (128, 1), 0) + (128 * c - KOFF)).astype(F32)
        before = uf[:, window] <= t
        start = jnp.max(jnp.where(before, last[:, window], -BIG), axis=1, keepdims=True)
        start = jnp.maximum(start, early)
        stop = jnp.min(jnp.where(before, BIG, first[:, window]), axis=1, keepdims=True)
        dprev[128 * c : 128 * c + 128, :] = jnp.broadcast_to(t - start, (128, 128))
        dnext[128 * c : 128 * c + 128, :] = jnp.broadcast_to(stop - t, (128, 128))


def attention_bias(dprev, dnext, bias):
    for i in range(F // 128):
        rows = slice(KOFF + 128 * i, KOFF + 128 * i + 128)
        back = dprev[rows, :].astype(jnp.int32)
        ahead = dnext[rows, :].astype(jnp.int32)
        rem = back & (BLOCK_LEN - 1)
        low = -jnp.minimum(back, rem + LEFT_BLOCKS * BLOCK_LEN)
        high = jnp.minimum(ahead, BLOCK_LEN - rem)
        for half in range(2):
            delta = (
                lax.broadcasted_iota(jnp.int32, (128, 128), 1)
                - lax.broadcasted_iota(jnp.int32, (128, 128), 0)
                + (128 * half - KOFF)
            )
            ok = (delta >= low) & (delta < high)
            bias[i, :, 128 * half : 128 * half + 128] = jnp.where(ok, F32(0.0), F32(-1e30))


def conv_norm(xf, taps, gain, dprev, dnext, hid, nrm, first, last, place_of):
    step = 64
    tiles = D // 128

    def block(n, _):
        r0, d0 = (pl.multiple_of(v, step) for v in place_of(n))
        back = dprev[pl.ds(r0, step), :]
        ahead = dnext[pl.ds(r0, step), :]
        keep = [back >= F32(4 - j) if j < 4 else ahead > F32(j - 4) for j in range(9)]
        hs = []
        total = jnp.zeros((step, 128), F32)
        for c in range(tiles):
            cols = slice(128 * c, 128 * c + 128)
            centre = xf[c, pl.ds(r0 + 16, step), :]
            acc = centre * taps[4:5, cols]
            for j in range(9):
                if j == 4:
                    continue
                term = xf[c, pl.ds(r0 + 12 + j, step), :] * taps[j : j + 1, cols]
                acc = acc + jnp.where(keep[j], term, F32(0.0))
            h16 = (centre + acc).astype(BF16)
            hid[pl.ds(r0, step), cols] = h16
            h = h16.astype(F32)
            hs.append(h)
            total = total + h
        mean = jnp.sum(total, axis=1, keepdims=True) * F32(1.0 / D)
        hs = [h - mean for h in hs]
        square = jnp.zeros((step, 128), F32)
        for h in hs:
            square = square + h * h
        var = jnp.sum(square, axis=1, keepdims=True) * F32(1.0 / D)
        scale = lax.rsqrt(var + F32(1e-5))
        for c in range(tiles):
            cols = slice(128 * c, 128 * c + 128)
            nrm[pl.ds(d0, step), cols] = (hs[c] * scale * gain[:, cols]).astype(BF16)
        return 0

    lax.fori_loop(first, last, block, 0)


def project(nrm, rows, weights, base, out, pieces):
    value = jnp.dot(
        nrm[rows, :], weights[:, base : base + D], preferred_element_type=F32
    ).astype(BF16)
    at = 0
    for place, size in pieces:
        out[place : place + size, :] = value[at : at + size]
        at += size


def attend(heads, tiles, q, k, v, bias, attn):
    factor = 1.4426950408889634 / 128.0**0.5
    work = []
    for h in heads:
        lanes = pl.ds(pl.multiple_of(h * 128, 128), 128)
        for i in tiles:
            own = slice(128 * i, 128 * i + 128)
            seen = slice(128 * i, 128 * i + 256)
            s = lax.dot_general(
                q[own, lanes], k[seen, lanes], (((1,), (1,)), ((), ())), preferred_element_type=F32
            )
            work.append((own, seen, lanes, s + bias[i]))
    tops = [jnp.max(s, axis=1, keepdims=True) for _, _, _, s in work]
    expos = [jnp.exp2((item[3] - top) * factor) for item, top in zip(work, tops)]
    norms = [1.0 / jnp.sum(e, axis=1, keepdims=True) for e in expos]
    for (own, seen, lanes, _), e, norm in zip(work, expos, norms):
        w = (e * norm).astype(BF16)
        attn[own, lanes] = jnp.dot(w, v[seen, lanes], preferred_element_type=F32).astype(BF16)


def placement_of(row):
    rows = row.shape[1]
    square = lax.broadcasted_iota(jnp.int32, (rows, rows), 0) == lax.broadcasted_iota(
        jnp.int32, (rows, rows), 1
    )
    spread = jnp.where(square, row.astype(F32), F32(0.0))
    owner = jnp.sum(spread, axis=1, keepdims=True).astype(jnp.int32)
    lane = lax.broadcasted_iota(jnp.int32, (rows, 128), 1)
    hot = jnp.where(owner == lane, F32(1.0), F32(0.0))
    lower = jnp.where(
        lax.broadcasted_iota(jnp.int32, (rows, rows), 1)
        < lax.broadcasted_iota(jnp.int32, (rows, rows), 0),
        F32(1.0),
        F32(0.0),
    ).astype(BF16)
    before = jnp.dot(lower, hot.astype(BF16), preferred_element_type=F32)
    rank = jnp.sum(hot * before, axis=1, keepdims=True).astype(jnp.int32)
    slot = owner * 4 + rank
    slot_row = jnp.sum(jnp.where(square, slot.astype(F32), F32(0.0)), axis=0, keepdims=True)
    column = lax.broadcasted_iota(jnp.int32, (128, rows), 0)
    by_slot = jnp.where(column == slot_row.astype(jnp.int32), F32(1.0), F32(0.0)).astype(BF16)
    by_row = jnp.where(lane == slot, F32(1.0), F32(0.0)).astype(BF16)
    return by_slot, by_row


def remote(src, dst, sends, recvs, index, target):
    return pltpu.make_async_remote_copy(
        src_ref=src,
        dst_ref=dst,
        send_sem=sends.at[index],
        recv_sem=recvs.at[index],
        device_id=target,
        device_id_type=MESH,
    )


def each(count, body):
    def one(k, _):
        body(k)
        return 0

    lax.fori_loop(1, count, one, 0)


def to_slots(value, wide, slots):
    for c in range(D // 128):
        wide[pl.ds(c, 128, stride=8), :] = value[:, 128 * c : 128 * c + 128].astype(F32)
    for o in range(N_SEQ):
        slots[o] = wide[32 * o : 32 * o + 32, :].astype(BF16)


def from_slots(slots, wide):
    for o in range(N_SEQ):
        wide[32 * o : 32 * o + 32, :] = slots[o].astype(F32)
    return [wide[pl.ds(c, 128, stride=8), :].astype(BF16) for c in range(D // 128)]


def whole_kernel(
    frames, begins, owner_hbm, taps_hbm, gain_hbm, wqkv_hbm, wout_hbm, cot_hbm,
    audio, fin,
    xb, xf, bgs, dprev, dnext, hid, nrm, edge, qs, ks, vs, bias, attn, wqkv, wout,
    cotv, cots, back, gall, wide, place, pick, ahl, asp, aall, part, tiles, got, aout, arecv,
    owner, taps, gain,
    local_sems, halo_s, halo_r, cot_s, cot_r, g_s, g_r, relay_s, relay_r, a_s, a_r, xz_s, xz_r,
    t_s, t_r, m_s, m_r, h0_s, h0_r, h1_s, h1_r, p0_s, p0_r, p1_s, p1_r, c_s, c_r,
):
    z = lax.axis_index("grp")
    s = lax.axis_index("seq")
    x = s // GROUP
    j = s % GROUP
    y = j // 2
    c = j % 2

    def seq(k):
        return {"seq": (s + k) % N_SEQ}

    def grp(k):
        return {"grp": (z + k) % N_GRP}

    def in_group(k):
        return {"seq": x * GROUP + (j + k) % GROUP}

    def along_x(k):
        return {"seq": (x + k) % N_X * GROUP + j}

    def along_y(k):
        return {"seq": x * GROUP + (y + k) % N_Y * 2 + c}

    other_core = {"seq": x * GROUP + y * 2 + (1 - c)}

    barrier = pltpu.get_barrier_semaphore()

    def greet(target):
        pl.semaphore_signal(barrier, inc=1, device_id=target, device_id_type=MESH)

    def across(k):
        return {"grp": (z + k % N_GRP) % N_GRP, "seq": (x + k // N_GRP) % N_X * GROUP + j}

    each(N_SEQ, lambda k: greet(seq(k)))

    def greet_planes(kz):
        for kx in range(N_X):
            greet(across(kx * N_GRP + kz))

    each(N_GRP, greet_planes)

    def rows_of(source):
        return pl.ds(pl.multiple_of(source * 64, 64), 64)

    loads = [
        pltpu.make_async_copy(begins, bgs.at[3], local_sems.at[0]),
        pltpu.make_async_copy(frames.at[0], xb.at[pl.ds(LEFT, F)], local_sems.at[1]),
        pltpu.make_async_copy(taps_hbm, taps, local_sems.at[2]),
        pltpu.make_async_copy(gain_hbm, gain, local_sems.at[3]),
        pltpu.make_async_copy(cot_hbm.at[0], cotv, local_sems.at[4]),
        pltpu.make_async_copy(owner_hbm, owner, local_sems.at[5]),
        pltpu.make_async_copy(wqkv_hbm, wqkv, local_sems.at[6]),
        pltpu.make_async_copy(wout_hbm, wout, local_sems.at[7]),
    ]
    for copy in loads:
        copy.start()
    for copy in loads[:4]:
        copy.wait()
    none = jnp.zeros((1, F), jnp.int32)
    alone = jnp.concatenate([none, none, none, bgs[3], none[:, :128]], axis=1)
    bounds(alone, s * F, F * N_SEQ, dprev, dnext)
    for tile in range(D // 128):
        xf[tile, LEFT : LEFT + F] = xb[LEFT : LEFT + F, 128 * tile : 128 * tile + 128].astype(F32)
    loads[4].wait()
    to_slots(cotv[...], wide, cots)
    inner = lambda n: (128 + 64 * n, 64 * n)
    conv_norm(xf, taps, gain, dprev, dnext, hid, nrm, 0, 4, inner)
    pl.semaphore_wait(barrier, N_SEQ - 1 + N_X * (N_GRP - 1))

    halo = [
        remote(frames.at[0, pl.ds(F - LEFT, LEFT)], xb.at[pl.ds(0, LEFT)], halo_s, halo_r, 0, seq(1)),
        remote(frames.at[0, pl.ds(0, RIGHT)], xb.at[pl.ds(LEFT + F, RIGHT)], halo_s, halo_r, 1, seq(N_SEQ - 1)),
        remote(begins, bgs.at[2], halo_s, halo_r, 2, seq(1)),
        remote(begins, bgs.at[1], halo_s, halo_r, 3, seq(2)),
        remote(begins, bgs.at[0], halo_s, halo_r, 4, seq(3)),
        remote(begins, bgs.at[4], halo_s, halo_r, 5, seq(N_SEQ - 1)),
    ]
    for copy in halo[2:]:
        copy.start()

    def copy_cot(k):
        return remote(cots.at[(s + k) % N_SEQ], back.at[s], cot_s, cot_r, k, seq(k))

    each(N_SEQ, lambda k: copy_cot(k).start())
    for copy in halo[:2]:
        copy.start()
    back[s] = cots[s]

    conv_norm(xf, taps, gain, dprev, dnext, hid, nrm, 4, 7, inner)
    loads[5].wait()
    place[...], pick[...] = placement_of(owner[...])
    loads[6].wait()
    project(nrm, slice(0, 448), wqkv, 0, qs, ((32, 448),))

    project(nrm, slice(0, 448), wqkv, D, ks, ((128, 448),))
    project(nrm, slice(0, 448), wqkv, 2 * D, vs, ((128, 448),))
    for copy in halo[2:]:
        copy.wait_recv()
    marks = jnp.concatenate([bgs[0], bgs[1], bgs[2], bgs[3], bgs[4][:, :128]], axis=1)
    bounds(marks, s * F, F * N_SEQ, dprev, dnext)
    attention_bias(dprev, dnext, bias)

    def got_cot(k):
        source = (s + N_SEQ - k) % N_SEQ
        remote(back.at[source], back.at[source], cot_s, cot_r, k, seq(k)).wait_recv()

    each(N_SEQ, got_cot)
    for tile, value in enumerate(from_slots(back, wide)):
        gall[rows_of(j), 128 * tile : 128 * tile + 128] = jnp.dot(
            pick[...], value, preferred_element_type=F32
        ).astype(BF16)

    def copy_g(k):
        block = gall.at[rows_of(j)]
        return remote(block, block, g_s, g_r, k, along_y(k))

    def copy_relay(k):
        block = gall.at[rows_of((y + N_Y - k) % N_Y * 2 + c)]
        return remote(block, block, relay_s, relay_r, k, other_core)

    for k in (1, 3, 2):
        copy_g(k).start()
    copy_relay(0).start()

    def middle(n, _):
        attend([4 * n + h for h in range(4)], (1, 2), qs, ks, vs, bias, attn)
        return 0

    lax.fori_loop(0, HEADS // 4, middle, 0)
    for copy in halo[:2]:
        copy.wait_recv()
    for tile in range(D // 128):
        cols = slice(128 * tile, 128 * tile + 128)
        xf[tile, :LEFT] = xb[:LEFT, cols].astype(F32)
        xf[tile, LEFT + F :] = xb[LEFT + F :, cols].astype(F32)
    conv_norm(
        xf, taps, gain, dprev, dnext, hid, edge, 0, 3,
        lambda n: (64 * n + 448 * (n // 2), 64 * n),
    )
    project(edge, slice(96, 160), wqkv, 0, qs, ((0, 32), (480, 32)))
    project(edge, slice(0, 192), wqkv, D, ks, ((0, 128), (576, 64)))
    project(edge, slice(0, 192), wqkv, 2 * D, vs, ((0, 128), (576, 64)))

    rows = F // SUB
    gather = jnp.where(
        lax.broadcasted_iota(jnp.int32, (rows, F), 1) >> 3
        == lax.broadcasted_iota(jnp.int32, (rows, F), 0),
        F32(1.0),
        F32(0.0),
    ).astype(BF16)

    def copy_a(n):
        return remote(asp.at[(j + n) % HEADS], aall.at[:, rows_of(j)], a_s, a_r, n, in_group(n))

    def two_heads(n, m):
        pair = ((j + n) % HEADS, (j + m) % HEADS)
        attend(pair, (0, 3), qs, ks, vs, bias, attn)
        for h in pair:
            lanes = pl.ds(pl.multiple_of(h * 128, 128), 128)
            asum = jnp.dot(gather, attn[:, lanes], preferred_element_type=F32)
            high = asum.astype(BF16)
            low = (asum - high.astype(F32)).astype(BF16)
            ahl[0, :, lanes] = high
            ahl[1, :, lanes] = low
            asp[h, 0] = high
            asp[h, 1] = low

    def two_heads_and_send(p, _):
        two_heads(2 * p + 1, 2 * p + 2)
        copy_a(2 * p + 1).start()
        copy_a(2 * p + 2).start()
        return 0

    lax.fori_loop(0, 3, two_heads_and_send, 0)
    two_heads(7, 0)
    copy_a(7).start()
    aall[:, rows_of(j), :] = asp[j]
    for k in (1, 3, 2):
        copy_g(k).wait_recv()
        copy_relay(k).start()

    loads[7].wait()
    hsum = jnp.dot(gather, hid[KOFF : KOFF + F, :], preferred_element_type=F32)
    proj = jnp.dot(ahl[0], wout[...], preferred_element_type=F32)
    proj = proj + jnp.dot(ahl[1], wout[...], preferred_element_type=F32)
    pooled = ((hsum + proj) * F32(1.0 / SUB)).astype(BF16)
    dims = (((0,), (0,)), ((), ()))
    outgoing = jnp.dot(place[...], pooled, preferred_element_type=F32)
    to_slots(outgoing, wide, aout)

    def copy_audio(k):
        return remote(aout.at[(s + k) % N_SEQ], arecv.at[s], m_s, m_r, k, seq(k))


    for k in range(N_Y):
        copy_relay(k).wait_recv()

    each(GROUP, lambda k: copy_a(k).wait_recv())
    part[...] = lax.dot_general(aall[0], gall[...], dims, preferred_element_type=F32)
    part[...] += lax.dot_general(aall[1], gall[...], dims, preferred_element_type=F32)
    for px in range(N_X):
        for pz in range(N_GRP):
            tiles[px, pz] = part[32 * px : 32 * px + 32, 128 * pz : 128 * pz + 128].astype(BF16)

    def copy_xz(k):
        block = tiles.at[(x + k // N_GRP) % N_X, (z + k % N_GRP) % N_GRP]
        return remote(block, got.at[k], xz_s, xz_r, k, across(k))

    each(N_X * N_GRP, lambda k: copy_xz(k).start())
    each(N_SEQ, lambda k: copy_audio(k).start())
    arecv[s] = aout[s]
    tile_sum = part[
        pl.ds(pl.multiple_of(x * 32, 32), 32), pl.ds(pl.multiple_of(z * 128, 128), 128)
    ]
    each(N_X * N_GRP, lambda k: copy_xz(k).wait_recv())
    for k in range(1, N_X * N_GRP):
        tile_sum = tile_sum + got[k].astype(F32)
    own_cols = pl.ds(pl.multiple_of(z * 128, 128), 128)
    fin[y, c, x, :, own_cols] = (tile_sum * F32(1.0 / (128 * SUB))).astype(BF16)

    def copy_t(k):
        tile = fin.at[y, c, x, :, own_cols]
        return remote(tile, tile, t_s, t_r, k, grp(k))

    for k in range(1, N_GRP):
        copy_t(k).start()
    for k in range(1, N_GRP):
        copy_t(k).wait_recv()

    first, second = pl.ds(0, D // 2), pl.ds(D // 2, D // 2)

    def copy_h0(k):
        block = fin.at[y, c, x, :, first]
        return remote(block, block, h0_s, h0_r, k, along_x(k))

    def copy_h1(k):
        block = fin.at[y, c, x, :, second]
        return remote(block, block, h1_s, h1_r, k, along_y(k))

    def copy_p0(kx, ky):
        block = fin.at[y, c, (x + N_X - kx) % N_X, :, first]
        return remote(block, block, p0_s, p0_r, kx * N_Y + ky, along_y(ky))

    def copy_p1(ky, kx):
        block = fin.at[(y + N_Y - ky) % N_Y, c, x, :, second]
        return remote(block, block, p1_s, p1_r, ky * N_X + kx, along_x(kx))

    def copy_c0(k):
        block = fin.at[(y + N_Y - k) % N_Y, c, :, :, first]
        return remote(block, block, c_s, c_r, k, other_core)

    def copy_c1(k):
        block = fin.at[:, c, (x + N_X - k) % N_X, :, second]
        return remote(block, block, c_s, c_r, N_Y + k, other_core)

    for k in (1, 3, 2):
        copy_h0(k).start()
        copy_h1(k).start()
    for k in (1, 3, 2):
        copy_p0(0, k).start()
        copy_p1(0, k).start()
    for k in (1, 3, 2):
        copy_h0(k).wait_recv()
        for ky in (1, 3, 2):
            copy_p0(k, ky).start()
        copy_h1(k).wait_recv()
        for kx in (1, 3, 2):
            copy_p1(k, kx).start()
    copy_c0(0).start()
    copy_c1(0).start()

    def got_audio(k):
        source = (s + N_SEQ - k) % N_SEQ
        remote(arecv.at[source], arecv.at[source], m_s, m_r, k, seq(k)).wait_recv()

    each(N_SEQ, got_audio)
    for tile, value in enumerate(from_slots(arecv, wide)):
        audio[:, 128 * tile : 128 * tile + 128] = value

    for k in (1, 3, 2):
        for other in range(N_X):
            copy_p0(other, k).wait_recv()
        copy_c0(k).start()
        for other in range(N_Y):
            copy_p1(other, k).wait_recv()
        copy_c1(k).start()
    for k in range(N_Y):
        copy_c0(k).wait_recv()
        copy_c1(k).wait_recv()

    for copy in halo:
        copy.wait_send()

    each(N_SEQ, lambda k: copy_audio(k).wait_send())

    each(N_SEQ, lambda k: copy_cot(k).wait_send())
    each(GROUP, lambda k: copy_a(k).wait_send())
    each(N_X * N_GRP, lambda k: copy_xz(k).wait_send())
    each(N_GRP, lambda k: copy_t(k).wait_send())
    for k in range(1, N_X):
        copy_g(k).wait_send()
        copy_h0(k).wait_send()
        copy_h1(k).wait_send()
    for k in range(N_Y):
        copy_relay(k).wait_send()
        copy_c0(k).wait_send()
        copy_c1(k).wait_send()
        for other in range(1, N_X):
            copy_p0(k, other).wait_send()
            copy_p1(k, other).wait_send()


def shards(frames, begins, owner, conv_kernel, norm_gain, w_qkv, w_out, cotangent):
    vm = pl.BlockSpec(memory_space=pltpu.VMEM)
    hbm = pl.BlockSpec(memory_space=pltpu.HBM)
    dma = pltpu.SemaphoreType.DMA
    audio, grad = pl.pallas_call(
        whole_kernel,
        out_shape=(
            jax.ShapeDtypeStruct((128, D), BF16),
            jax.ShapeDtypeStruct((N_Y, 2, N_X, 32, D), BF16),
        ),
        in_specs=[hbm] * 8,
        out_specs=(vm, vm),
        scratch_shapes=[
            pltpu.VMEM((LEFT + F + RIGHT, D), BF16),
            pltpu.VMEM((8, LEFT + F + RIGHT, 128), F32),
            pltpu.VMEM((5, 1, F), jnp.int32),
            pltpu.VMEM((KV, 128), F32),
            pltpu.VMEM((KV, 128), F32),
            pltpu.VMEM((KV, D), BF16),
            pltpu.VMEM((448, D), BF16),
            pltpu.VMEM((192, D), BF16),
            pltpu.VMEM((F, D), BF16),
            pltpu.VMEM((KV, D), BF16),
            pltpu.VMEM((KV, D), BF16),
            pltpu.VMEM((4, 128, 256), F32),
            pltpu.VMEM((F, D), BF16),
            pltpu.VMEM((D, 3 * D), BF16),
            pltpu.VMEM((D, D), BF16),
            pltpu.VMEM((128, D), BF16),
            pltpu.VMEM((N_SEQ, 32, 128), BF16),
            pltpu.VMEM((N_SEQ, 32, 128), BF16),
            pltpu.VMEM((GROUP * 64, D), BF16),
            pltpu.VMEM((1024, 128), F32),
            pltpu.VMEM((128, 64), BF16),
            pltpu.VMEM((64, 128), BF16),
            pltpu.VMEM((2, 64, D), BF16),
            pltpu.VMEM((HEADS, 2, 64, 128), BF16),
            pltpu.VMEM((2, GROUP * 64, 128), BF16),
            pltpu.VMEM((128, D), F32),
            pltpu.VMEM((N_X, N_GRP, 32, 128), BF16),
            pltpu.VMEM((N_X * N_GRP, 32, 128), BF16),
            pltpu.VMEM((N_SEQ, 32, 128), BF16),
            pltpu.VMEM((N_SEQ, 32, 128), BF16),
            pltpu.VMEM((1, 64), jnp.int32),
            pltpu.VMEM((9, D), F32),
            pltpu.VMEM((1, D), F32),
            dma((8,)),
            dma((6,)), dma((6,)),
            dma((N_SEQ,)), dma((N_SEQ,)),
            dma((N_Y,)), dma((N_Y,)),
            dma((N_Y,)), dma((N_Y,)),
            dma((GROUP,)), dma((GROUP,)),
            dma((N_X * N_GRP,)), dma((N_X * N_GRP,)),
            dma((N_GRP,)), dma((N_GRP,)),
            dma((N_SEQ,)), dma((N_SEQ,)),
            dma((N_X,)), dma((N_X,)),
            dma((N_Y,)), dma((N_Y,)),
            dma((N_X * N_Y,)), dma((N_X * N_Y,)),
            dma((N_X * N_Y,)), dma((N_X * N_Y,)),
            dma((2 * N_Y,)), dma((2 * N_Y,)),
        ],
        compiler_params=pltpu.CompilerParams(
            vmem_limit_bytes=48 * 1024 * 1024, collective_id=0, has_side_effects=True
        ),
        name="whole",
    )(
        *(
            pltpu.with_memory_space_constraint(value, pltpu.HBM)
            for value in (
                frames,
                begins,
                owner.reshape(1, 64),
                conv_kernel,
                norm_gain.reshape(1, D),
                w_qkv,
                w_out,
                cotangent,
            )
        )
    )
    return audio.reshape(1, 128, D), grad.reshape(D, D)


def solution(mesh):
    return jax.shard_map(
        shards,
        mesh=mesh,
        in_specs=(
            P("grp", "seq", None),
            P("grp", "seq"),
            P("grp", "seq", None),
            P(),
            P(),
            P(),
            P(),
            P("grp", "seq", None),
        ),
        out_specs=(P("grp", "seq", None), P()),
        check_vma=False,
    )
```

```python
import jax
import jax.numpy as jnp
from jax import lax
from jax.experimental import pallas as pl
from jax.experimental.pallas import tpu as pltpu
from jax.sharding import PartitionSpec as P

HEADS = 8
BLOCK_LEN = 32
LEFT_BLOCKS = 2
SUB = 8
F = 512
D = 1024
LEFT = 112
RIGHT = 48
KV = 640
KOFF = 96
FAR = 1536
BIG = 1e6
F32 = jnp.float32
BF16 = jnp.bfloat16
MESH = pl.DeviceIdType.MESH
N_SEQ = 32
N_GRP = 8
N_X = 4
N_Y = 4
GROUP = 8


def bounds(bg, t0, group_len, dprev, dnext):
    lanes = FAR + F + 128
    u = lax.broadcasted_iota(jnp.int32, (1, lanes), 1) - FAR
    at = u + t0
    mark = ((bg == 1) & (at >= 0)) | (at == group_len)
    uf = u.astype(F32)
    last = jnp.where(mark, uf, -BIG)
    first = jnp.where(mark, uf, BIG)
    for c in range(KV // 128):
        window = slice(FAR - 128 + 128 * c, FAR + 128 + 128 * c)
        early = jnp.max(last[:, : FAR - 128 + 128 * c], axis=1, keepdims=True)
        t = (lax.broadcasted_iota(jnp.int32, (128, 1), 0) + (128 * c - KOFF)).astype(F32)
        before = uf[:, window] <= t
        start = jnp.max(jnp.where(before, last[:, window], -BIG), axis=1, keepdims=True)
        start = jnp.maximum(start, early)
        stop = jnp.min(jnp.where(before, BIG, first[:, window]), axis=1, keepdims=True)
        dprev[128 * c : 128 * c + 128, :] = jnp.broadcast_to(t - start, (128, 128))
        dnext[128 * c : 128 * c + 128, :] = jnp.broadcast_to(stop - t, (128, 128))


def attention_bias(dprev, dnext, bias):
    for i in range(F // 128):
        rows = slice(KOFF + 128 * i, KOFF + 128 * i + 128)
        back = dprev[rows, :].astype(jnp.int32)
        ahead = dnext[rows, :].astype(jnp.int32)
        rem = back & (BLOCK_LEN - 1)
        low = -jnp.minimum(back, rem + LEFT_BLOCKS * BLOCK_LEN)
        high = jnp.minimum(ahead, BLOCK_LEN - rem)
        for half in range(2):
            delta = (
                lax.broadcasted_iota(jnp.int32, (128, 128), 1)
                - lax.broadcasted_iota(jnp.int32, (128, 128), 0)
                + (128 * half - KOFF)
            )
            ok = (delta >= low) & (delta < high)
            bias[i, :, 128 * half : 128 * half + 128] = jnp.where(ok, F32(0.0), F32(-1e30))


def conv_norm(xf, taps, gain, dprev, dnext, hid, nrm, first, last, place_of):
    step = 64
    tiles = D // 128

    def block(n, _):
        r0, d0 = (pl.multiple_of(v, step) for v in place_of(n))
        back = dprev[pl.ds(r0, step), :]
        ahead = dnext[pl.ds(r0, step), :]
        keep = [back >= F32(4 - j) if j < 4 else ahead > F32(j - 4) for j in range(9)]
        hs = []
        total = jnp.zeros((step, 128), F32)
        for c in range(tiles):
            cols = slice(128 * c, 128 * c + 128)
            centre = xf[c, pl.ds(r0 + 16, step), :]
            acc = centre * taps[4:5, cols]
            for j in range(9):
                if j == 4:
                    continue
                term = xf[c, pl.ds(r0 + 12 + j, step), :] * taps[j : j + 1, cols]
                acc = acc + jnp.where(keep[j], term, F32(0.0))
            h16 = (centre + acc).astype(BF16)
            hid[pl.ds(r0, step), cols] = h16
            h = h16.astype(F32)
            hs.append(h)
            total = total + h
        mean = jnp.sum(total, axis=1, keepdims=True) * F32(1.0 / D)
        hs = [h - mean for h in hs]
        square = jnp.zeros((step, 128), F32)
        for h in hs:
            square = square + h * h
        var = jnp.sum(square, axis=1, keepdims=True) * F32(1.0 / D)
        scale = lax.rsqrt(var + F32(1e-5))
        for c in range(tiles):
            cols = slice(128 * c, 128 * c + 128)
            nrm[pl.ds(d0, step), cols] = (hs[c] * scale * gain[:, cols]).astype(BF16)
        return 0

    lax.fori_loop(first, last, block, 0)


def project(nrm, rows, weights, base, out, pieces):
    value = jnp.dot(
        nrm[rows, :], weights[:, base : base + D], preferred_element_type=F32
    ).astype(BF16)
    at = 0
    for place, size in pieces:
        out[place : place + size, :] = value[at : at + size]
        at += size


def attend(heads, tiles, q, k, v, bias, attn):
    factor = 1.4426950408889634 / 128.0**0.5
    work = []
    for h in heads:
        lanes = pl.ds(pl.multiple_of(h * 128, 128), 128)
        for i in tiles:
            own = slice(128 * i, 128 * i + 128)
            seen = slice(128 * i, 128 * i + 256)
            s = lax.dot_general(
                q[own, lanes], k[seen, lanes], (((1,), (1,)), ((), ())), preferred_element_type=F32
            )
            work.append((own, seen, lanes, s + bias[i]))
    tops = [jnp.max(s, axis=1, keepdims=True) for _, _, _, s in work]
    expos = [jnp.exp2((item[3] - top) * factor) for item, top in zip(work, tops)]
    norms = [1.0 / jnp.sum(e, axis=1, keepdims=True) for e in expos]
    for (own, seen, lanes, _), e, norm in zip(work, expos, norms):
        w = (e * norm).astype(BF16)
        attn[own, lanes] = jnp.dot(w, v[seen, lanes], preferred_element_type=F32).astype(BF16)


def placement_of(row):
    rows = row.shape[1]
    square = lax.broadcasted_iota(jnp.int32, (rows, rows), 0) == lax.broadcasted_iota(
        jnp.int32, (rows, rows), 1
    )
    spread = jnp.where(square, row.astype(F32), F32(0.0))
    owner = jnp.sum(spread, axis=1, keepdims=True).astype(jnp.int32)
    lane = lax.broadcasted_iota(jnp.int32, (rows, 128), 1)
    hot = jnp.where(owner == lane, F32(1.0), F32(0.0))
    lower = jnp.where(
        lax.broadcasted_iota(jnp.int32, (rows, rows), 1)
        < lax.broadcasted_iota(jnp.int32, (rows, rows), 0),
        F32(1.0),
        F32(0.0),
    ).astype(BF16)
    before = jnp.dot(lower, hot.astype(BF16), preferred_element_type=F32)
    rank = jnp.sum(hot * before, axis=1, keepdims=True).astype(jnp.int32)
    slot = owner * 4 + rank
    slot_row = jnp.sum(jnp.where(square, slot.astype(F32), F32(0.0)), axis=0, keepdims=True)
    column = lax.broadcasted_iota(jnp.int32, (128, rows), 0)
    by_slot = jnp.where(column == slot_row.astype(jnp.int32), F32(1.0), F32(0.0)).astype(BF16)
    by_row = jnp.where(lane == slot, F32(1.0), F32(0.0)).astype(BF16)
    return by_slot, by_row


def remote(src, dst, sends, recvs, index, target):
    return pltpu.make_async_remote_copy(
        src_ref=src,
        dst_ref=dst,
        send_sem=sends.at[index],
        recv_sem=recvs.at[index],
        device_id=target,
        device_id_type=MESH,
    )


def each(count, body):
    def one(k, _):
        body(k)
        return 0

    lax.fori_loop(1, count, one, 0)


def to_slots(value, wide, slots):
    for c in range(D // 128):
        wide[pl.ds(c, 128, stride=8), :] = value[:, 128 * c : 128 * c + 128].astype(F32)
    for o in range(N_SEQ):
        slots[o] = wide[32 * o : 32 * o + 32, :].astype(BF16)


def from_slots(slots, wide):
    for o in range(N_SEQ):
        wide[32 * o : 32 * o + 32, :] = slots[o].astype(F32)
    return [wide[pl.ds(c, 128, stride=8), :].astype(BF16) for c in range(D // 128)]


def whole_kernel(
    frames, begins, owner_hbm, taps_hbm, gain_hbm, wqkv_hbm, wout_hbm, cot_hbm,
    audio, fin,
    xb, xf, bgs, dprev, dnext, hid, nrm, edge, qs, ks, vs, bias, attn, wqkv, wout,
    cotv, cots, back, gall, wide, place, pick, ahl, asp, aall, part, tiles, got, aout, arecv,
    owner, taps, gain,
    local_sems, halo_s, halo_r, cot_s, cot_r, g_s, g_r, relay_s, relay_r, a_s, a_r, xz_s, xz_r,
    t_s, t_r, m_s, m_r, h0_s, h0_r, h1_s, h1_r, p0_s, p0_r, p1_s, p1_r, c_s, c_r,
):
    z = lax.axis_index("grp")
    s = lax.axis_index("seq")
    x = s // GROUP
    j = s % GROUP
    y = j // 2
    c = j % 2

    def seq(k):
        return {"seq": (s + k) % N_SEQ}

    def grp(k):
        return {"grp": (z + k) % N_GRP}

    def in_group(k):
        return {"seq": x * GROUP + (j + k) % GROUP}

    def along_x(k):
        return {"seq": (x + k) % N_X * GROUP + j}

    def along_y(k):
        return {"seq": x * GROUP + (y + k) % N_Y * 2 + c}

    other_core = {"seq": x * GROUP + y * 2 + (1 - c)}

    barrier = pltpu.get_barrier_semaphore()

    def greet(target):
        pl.semaphore_signal(barrier, inc=1, device_id=target, device_id_type=MESH)

    def across(k):
        return {"grp": (z + k % N_GRP) % N_GRP, "seq": (x + k // N_GRP) % N_X * GROUP + j}

    each(N_SEQ, lambda k: greet(seq(k)))

    def greet_planes(kz):
        for kx in range(N_X):
            greet(across(kx * N_GRP + kz))

    each(N_GRP, greet_planes)

    def rows_of(source):
        return pl.ds(pl.multiple_of(source * 64, 64), 64)

    loads = [
        pltpu.make_async_copy(begins, bgs.at[3], local_sems.at[0]),
        pltpu.make_async_copy(frames.at[0], xb.at[pl.ds(LEFT, F)], local_sems.at[1]),
        pltpu.make_async_copy(taps_hbm, taps, local_sems.at[2]),
        pltpu.make_async_copy(gain_hbm, gain, local_sems.at[3]),
        pltpu.make_async_copy(cot_hbm.at[0], cotv, local_sems.at[4]),
        pltpu.make_async_copy(owner_hbm, owner, local_sems.at[5]),
        pltpu.make_async_copy(wqkv_hbm, wqkv, local_sems.at[6]),
        pltpu.make_async_copy(wout_hbm, wout, local_sems.at[7]),
    ]
    for copy in loads:
        copy.start()
    for copy in loads[:4]:
        copy.wait()
    none = jnp.zeros((1, F), jnp.int32)
    alone = jnp.concatenate([none, none, none, bgs[3], none[:, :128]], axis=1)
    bounds(alone, s * F, F * N_SEQ, dprev, dnext)
    for tile in range(D // 128):
        xf[tile, LEFT : LEFT + F] = xb[LEFT : LEFT + F, 128 * tile : 128 * tile + 128].astype(F32)
    loads[4].wait()
    to_slots(cotv[...], wide, cots)
    inner = lambda n: (128 + 64 * n, 64 * n)
    conv_norm(xf, taps, gain, dprev, dnext, hid, nrm, 0, 2, inner)
    pl.semaphore_wait(barrier, N_SEQ - 1 + N_X * (N_GRP - 1))

    halo = [
        remote(frames.at[0, pl.ds(F - LEFT, LEFT)], xb.at[pl.ds(0, LEFT)], halo_s, halo_r, 0, seq(1)),
        remote(frames.at[0, pl.ds(0, RIGHT)], xb.at[pl.ds(LEFT + F, RIGHT)], halo_s, halo_r, 1, seq(N_SEQ - 1)),
        remote(begins, bgs.at[2], halo_s, halo_r, 2, seq(1)),
        remote(begins, bgs.at[1], halo_s, halo_r, 3, seq(2)),
        remote(begins, bgs.at[0], halo_s, halo_r, 4, seq(3)),
        remote(begins, bgs.at[4], halo_s, halo_r, 5, seq(N_SEQ - 1)),
    ]
    for copy in halo[2:]:
        copy.start()

    def copy_cot(k):
        return remote(cots.at[(s + k) % N_SEQ], back.at[s], cot_s, cot_r, k, seq(k))

    each(N_SEQ, lambda k: copy_cot(k).start())
    for copy in halo[:2]:
        copy.start()
    back[s] = cots[s]

    conv_norm(xf, taps, gain, dprev, dnext, hid, nrm, 2, 7, inner)
    loads[5].wait()
    place[...], pick[...] = placement_of(owner[...])
    loads[6].wait()
    project(nrm, slice(0, 448), wqkv, 0, qs, ((32, 448),))

    project(nrm, slice(0, 448), wqkv, D, ks, ((128, 448),))
    project(nrm, slice(0, 448), wqkv, 2 * D, vs, ((128, 448),))
    for copy in halo[2:]:
        copy.wait_recv()
    marks = jnp.concatenate([bgs[0], bgs[1], bgs[2], bgs[3], bgs[4][:, :128]], axis=1)
    bounds(marks, s * F, F * N_SEQ, dprev, dnext)
    attention_bias(dprev, dnext, bias)

    def middle(n, _):
        attend([4 * n + h for h in range(4)], (1, 2), qs, ks, vs, bias, attn)
        return 0

    lax.fori_loop(0, 1, middle, 0)

    def got_cot(k):
        source = (s + N_SEQ - k) % N_SEQ
        remote(back.at[source], back.at[source], cot_s, cot_r, k, seq(k)).wait_recv()

    each(N_SEQ, got_cot)
    for tile, value in enumerate(from_slots(back, wide)):
        gall[rows_of(j), 128 * tile : 128 * tile + 128] = jnp.dot(
            pick[...], value, preferred_element_type=F32
        ).astype(BF16)

    def copy_g(k):
        block = gall.at[rows_of(j)]
        return remote(block, block, g_s, g_r, k, along_y(k))

    def copy_relay(k):
        block = gall.at[rows_of((y + N_Y - k) % N_Y * 2 + c)]
        return remote(block, block, relay_s, relay_r, k, other_core)

    for k in (1, 3, 2):
        copy_g(k).start()
    copy_relay(0).start()

    lax.fori_loop(1, HEADS // 4, middle, 0)
    for copy in halo[:2]:
        copy.wait_recv()
    for tile in range(D // 128):
        cols = slice(128 * tile, 128 * tile + 128)
        xf[tile, :LEFT] = xb[:LEFT, cols].astype(F32)
        xf[tile, LEFT + F :] = xb[LEFT + F :, cols].astype(F32)
    conv_norm(
        xf, taps, gain, dprev, dnext, hid, edge, 0, 3,
        lambda n: (64 * n + 448 * (n // 2), 64 * n),
    )
    project(edge, slice(96, 160), wqkv, 0, qs, ((0, 32), (480, 32)))
    project(edge, slice(0, 192), wqkv, D, ks, ((0, 128), (576, 64)))
    project(edge, slice(0, 192), wqkv, 2 * D, vs, ((0, 128), (576, 64)))

    rows = F // SUB
    gather = jnp.where(
        lax.broadcasted_iota(jnp.int32, (rows, F), 1) >> 3
        == lax.broadcasted_iota(jnp.int32, (rows, F), 0),
        F32(1.0),
        F32(0.0),
    ).astype(BF16)

    def copy_a(n):
        return remote(asp.at[(j + n) % HEADS], aall.at[rows_of(j)], a_s, a_r, n, in_group(n))

    def some_heads(*turns):
        pair = [(j + n) % HEADS for n in turns]
        attend(pair, (0, 3), qs, ks, vs, bias, attn)
        for h in pair:
            lanes = pl.ds(pl.multiple_of(h * 128, 128), 128)
            asum = jnp.dot(gather, attn[:, lanes], preferred_element_type=F32)
            high = asum.astype(BF16)
            low = (asum - high.astype(F32)).astype(BF16)
            ahl[:rows, lanes] = high
            ahl[rows:, lanes] = low
            asp[h, :, :128] = high
            asp[h, :, 128:] = low

    def two_heads_and_send(p, _):
        some_heads(2 * p + 1, 2 * p + 2)
        copy_a(2 * p + 1).start()
        copy_a(2 * p + 2).start()
        return 0

    lax.fori_loop(0, 2, two_heads_and_send, 0)
    some_heads(5, 6, 7)
    for n in (5, 6, 7):
        copy_a(n).start()
    some_heads(0)
    aall[rows_of(j), :] = asp[j]
    for k in (1, 3, 2):
        copy_g(k).wait_recv()
        copy_relay(k).start()

    loads[7].wait()
    hsum = jnp.dot(gather, hid[KOFF : KOFF + F, :], preferred_element_type=F32)
    proj = jnp.dot(ahl[...], wout[...], preferred_element_type=F32)
    proj = proj[:rows] + proj[rows:]
    pooled = ((hsum + proj) * F32(1.0 / SUB)).astype(BF16)
    dims = (((0,), (0,)), ((), ()))
    outgoing = jnp.dot(place[...], pooled, preferred_element_type=F32)
    to_slots(outgoing, wide, aout)

    def copy_audio(k):
        return remote(aout.at[(s + k) % N_SEQ], arecv.at[s], m_s, m_r, k, seq(k))


    for k in range(N_Y):
        copy_relay(k).wait_recv()

    each(GROUP, lambda k: copy_a(k).wait_recv())
    both = lax.dot_general(aall[...], gall[...], dims, preferred_element_type=F32)
    part[...] = both[:128] + both[128:]
    for px in range(N_X):
        for pz in range(N_GRP):
            tiles[px, pz] = part[32 * px : 32 * px + 32, 128 * pz : 128 * pz + 128].astype(BF16)

    def copy_xz(k):
        block = tiles.at[(x + k // N_GRP) % N_X, (z + k % N_GRP) % N_GRP]
        return remote(block, got.at[k], xz_s, xz_r, k, across(k))

    far_first = (4, 3, 5, 2, 6, 1, 7)
    for kz in far_first:
        for kx in range(N_X):
            copy_xz(kx * N_GRP + kz).start()
    for kx in range(1, N_X):
        copy_xz(kx * N_GRP).start()
    each(N_SEQ, lambda k: copy_audio(k).start())
    arecv[s] = aout[s]
    tile_sum = part[
        pl.ds(pl.multiple_of(x * 32, 32), 32), pl.ds(pl.multiple_of(z * 128, 128), 128)
    ]
    each(N_X * N_GRP, lambda k: copy_xz(k).wait_recv())
    for k in range(1, N_X * N_GRP):
        tile_sum = tile_sum + got[k].astype(F32)
    own_cols = pl.ds(pl.multiple_of(z * 128, 128), 128)
    fin[y, c, x, :, own_cols] = (tile_sum * F32(1.0 / (128 * SUB))).astype(BF16)

    def copy_t(k):
        tile = fin.at[y, c, x, :, own_cols]
        return remote(tile, tile, t_s, t_r, k, grp(k))

    for k in far_first:
        copy_t(k).start()
    for k in range(1, N_GRP):
        copy_t(k).wait_recv()

    first, second = pl.ds(0, D // 2), pl.ds(D // 2, D // 2)

    def copy_h0(k):
        block = fin.at[y, c, x, :, first]
        return remote(block, block, h0_s, h0_r, k, along_x(k))

    def copy_h1(k):
        block = fin.at[y, c, x, :, second]
        return remote(block, block, h1_s, h1_r, k, along_y(k))

    def copy_p0(kx, ky):
        block = fin.at[y, c, (x + N_X - kx) % N_X, :, first]
        return remote(block, block, p0_s, p0_r, kx * N_Y + ky, along_y(ky))

    def copy_p1(ky, kx):
        block = fin.at[(y + N_Y - ky) % N_Y, c, x, :, second]
        return remote(block, block, p1_s, p1_r, ky * N_X + kx, along_x(kx))

    def copy_c0(k):
        block = fin.at[(y + N_Y - k) % N_Y, c, :, :, first]
        return remote(block, block, c_s, c_r, k, other_core)

    def copy_c1(k):
        block = fin.at[:, c, (x + N_X - k) % N_X, :, second]
        return remote(block, block, c_s, c_r, N_Y + k, other_core)

    for k in (1, 3, 2):
        copy_h0(k).start()
        copy_h1(k).start()
    for k in (1, 3, 2):
        copy_p0(0, k).start()
        copy_p1(0, k).start()
    for k in (1, 3, 2):
        copy_h0(k).wait_recv()
        for ky in (1, 3, 2):
            copy_p0(k, ky).start()
        copy_h1(k).wait_recv()
        for kx in (1, 3, 2):
            copy_p1(k, kx).start()
    copy_c0(0).start()
    copy_c1(0).start()

    def got_audio(k):
        source = (s + N_SEQ - k) % N_SEQ
        remote(arecv.at[source], arecv.at[source], m_s, m_r, k, seq(k)).wait_recv()

    each(N_SEQ, got_audio)
    for tile, value in enumerate(from_slots(arecv, wide)):
        audio[:, 128 * tile : 128 * tile + 128] = value

    for k in (1, 3, 2):
        for other in range(N_X):
            copy_p0(other, k).wait_recv()
        copy_c0(k).start()
        for other in range(N_Y):
            copy_p1(other, k).wait_recv()
        copy_c1(k).start()
    for k in range(N_Y):
        copy_c0(k).wait_recv()
        copy_c1(k).wait_recv()

    for copy in halo:
        copy.wait_send()

    each(N_SEQ, lambda k: copy_audio(k).wait_send())

    each(N_SEQ, lambda k: copy_cot(k).wait_send())
    each(GROUP, lambda k: copy_a(k).wait_send())
    each(N_X * N_GRP, lambda k: copy_xz(k).wait_send())
    each(N_GRP, lambda k: copy_t(k).wait_send())
    for k in range(1, N_X):
        copy_g(k).wait_send()
        copy_h0(k).wait_send()
        copy_h1(k).wait_send()
    for k in range(N_Y):
        copy_relay(k).wait_send()
        copy_c0(k).wait_send()
        copy_c1(k).wait_send()
        for other in range(1, N_X):
            copy_p0(k, other).wait_send()
            copy_p1(k, other).wait_send()


def shards(frames, begins, owner, conv_kernel, norm_gain, w_qkv, w_out, cotangent):
    vm = pl.BlockSpec(memory_space=pltpu.VMEM)
    hbm = pl.BlockSpec(memory_space=pltpu.HBM)
    dma = pltpu.SemaphoreType.DMA
    audio, grad = pl.pallas_call(
        whole_kernel,
        out_shape=(
            jax.ShapeDtypeStruct((128, D), BF16),
            jax.ShapeDtypeStruct((N_Y, 2, N_X, 32, D), BF16),
        ),
        in_specs=[hbm] * 8,
        out_specs=(vm, vm),
        scratch_shapes=[
            pltpu.VMEM((LEFT + F + RIGHT, D), BF16),
            pltpu.VMEM((8, LEFT + F + RIGHT, 128), F32),
            pltpu.VMEM((5, 1, F), jnp.int32),
            pltpu.VMEM((KV, 128), F32),
            pltpu.VMEM((KV, 128), F32),
            pltpu.VMEM((KV, D), BF16),
            pltpu.VMEM((448, D), BF16),
            pltpu.VMEM((192, D), BF16),
            pltpu.VMEM((F, D), BF16),
            pltpu.VMEM((KV, D), BF16),
            pltpu.VMEM((KV, D), BF16),
            pltpu.VMEM((4, 128, 256), F32),
            pltpu.VMEM((F, D), BF16),
            pltpu.VMEM((D, 3 * D), BF16),
            pltpu.VMEM((D, D), BF16),
            pltpu.VMEM((128, D), BF16),
            pltpu.VMEM((N_SEQ, 32, 128), BF16),
            pltpu.VMEM((N_SEQ, 32, 128), BF16),
            pltpu.VMEM((GROUP * 64, D), BF16),
            pltpu.VMEM((1024, 128), F32),
            pltpu.VMEM((128, 64), BF16),
            pltpu.VMEM((64, 128), BF16),
            pltpu.VMEM((128, D), BF16),
            pltpu.VMEM((HEADS, 64, 256), BF16),
            pltpu.VMEM((GROUP * 64, 256), BF16),
            pltpu.VMEM((128, D), F32),
            pltpu.VMEM((N_X, N_GRP, 32, 128), BF16),
            pltpu.VMEM((N_X * N_GRP, 32, 128), BF16),
            pltpu.VMEM((N_SEQ, 32, 128), BF16),
            pltpu.VMEM((N_SEQ, 32, 128), BF16),
            pltpu.VMEM((1, 64), jnp.int32),
            pltpu.VMEM((9, D), F32),
            pltpu.VMEM((1, D), F32),
            dma((8,)),
            dma((6,)), dma((6,)),
            dma((N_SEQ,)), dma((N_SEQ,)),
            dma((N_Y,)), dma((N_Y,)),
            dma((N_Y,)), dma((N_Y,)),
            dma((GROUP,)), dma((GROUP,)),
            dma((N_X * N_GRP,)), dma((N_X * N_GRP,)),
            dma((N_GRP,)), dma((N_GRP,)),
            dma((N_SEQ,)), dma((N_SEQ,)),
            dma((N_X,)), dma((N_X,)),
            dma((N_Y,)), dma((N_Y,)),
            dma((N_X * N_Y,)), dma((N_X * N_Y,)),
            dma((N_X * N_Y,)), dma((N_X * N_Y,)),
            dma((2 * N_Y,)), dma((2 * N_Y,)),
        ],
        compiler_params=pltpu.CompilerParams(
            vmem_limit_bytes=48 * 1024 * 1024, collective_id=0, has_side_effects=True
        ),
        name="whole",
    )(
        *(
            pltpu.with_memory_space_constraint(value, pltpu.HBM)
            for value in (
                frames,
                begins,
                owner.reshape(1, 64),
                conv_kernel,
                norm_gain.reshape(1, D),
                w_qkv,
                w_out,
                cotangent,
            )
        )
    )
    return audio.reshape(1, 128, D), grad.reshape(D, D)


def solution(mesh):
    return jax.shard_map(
        shards,
        mesh=mesh,
        in_specs=(
            P("grp", "seq", None),
            P("grp", "seq"),
            P("grp", "seq", None),
            P(),
            P(),
            P(),
            P(),
            P("grp", "seq", None),
        ),
        out_specs=(P("grp", "seq", None), P()),
        check_vma=False,
    )
```

```python
import jax
import jax.numpy as jnp
from jax import lax
from jax.experimental import pallas as pl
from jax.experimental.pallas import tpu as pltpu
from jax.sharding import PartitionSpec as P

HEADS = 8
BLOCK_LEN = 32
LEFT_BLOCKS = 2
SUB = 8
F = 512
D = 1024
LEFT = 112
RIGHT = 48
KV = 640
KOFF = 96
FAR = 1536
BIG = 1e6
F32 = jnp.float32
BF16 = jnp.bfloat16
MESH = pl.DeviceIdType.MESH
N_SEQ = 32
N_GRP = 8
N_X = 4
N_Y = 4
GROUP = 8


def bounds(bg, t0, group_len, dprev, dnext):
    lanes = FAR + F + 128
    u = lax.broadcasted_iota(jnp.int32, (1, lanes), 1) - FAR
    at = u + t0
    mark = ((bg == 1) & (at >= 0)) | (at == group_len)
    uf = u.astype(F32)
    last = jnp.where(mark, uf, -BIG)
    first = jnp.where(mark, uf, BIG)
    for c in range(KV // 128):
        window = slice(FAR - 128 + 128 * c, FAR + 128 + 128 * c)
        early = jnp.max(last[:, : FAR - 128 + 128 * c], axis=1, keepdims=True)
        t = (lax.broadcasted_iota(jnp.int32, (128, 1), 0) + (128 * c - KOFF)).astype(F32)
        before = uf[:, window] <= t
        start = jnp.max(jnp.where(before, last[:, window], -BIG), axis=1, keepdims=True)
        start = jnp.maximum(start, early)
        stop = jnp.min(jnp.where(before, BIG, first[:, window]), axis=1, keepdims=True)
        dprev[128 * c : 128 * c + 128, :] = jnp.broadcast_to(t - start, (128, 128))
        dnext[128 * c : 128 * c + 128, :] = jnp.broadcast_to(stop - t, (128, 128))


def attention_bias(dprev, dnext, bias):
    for i in range(F // 128):
        rows = slice(KOFF + 128 * i, KOFF + 128 * i + 128)
        back = dprev[rows, :].astype(jnp.int32)
        ahead = dnext[rows, :].astype(jnp.int32)
        rem = back & (BLOCK_LEN - 1)
        low = -jnp.minimum(back, rem + LEFT_BLOCKS * BLOCK_LEN)
        high = jnp.minimum(ahead, BLOCK_LEN - rem)
        for half in range(2):
            delta = (
                lax.broadcasted_iota(jnp.int32, (128, 128), 1)
                - lax.broadcasted_iota(jnp.int32, (128, 128), 0)
                + (128 * half - KOFF)
            )
            ok = (delta >= low) & (delta < high)
            bias[i, :, 128 * half : 128 * half + 128] = jnp.where(ok, F32(0.0), F32(-1e30))


def conv_norm(xf, taps, gain, dprev, dnext, hid, nrm, first, last, place_of):
    step = 64
    tiles = D // 128

    def block(n, _):
        r0, d0 = (pl.multiple_of(v, step) for v in place_of(n))
        back = dprev[pl.ds(r0, step), :]
        ahead = dnext[pl.ds(r0, step), :]
        keep = [back >= F32(4 - j) if j < 4 else ahead > F32(j - 4) for j in range(9)]
        hs = []
        total = jnp.zeros((step, 128), F32)
        for c in range(tiles):
            cols = slice(128 * c, 128 * c + 128)
            centre = xf[c, pl.ds(r0 + 16, step), :]
            acc = centre * taps[4:5, cols]
            for j in range(9):
                if j == 4:
                    continue
                term = xf[c, pl.ds(r0 + 12 + j, step), :] * taps[j : j + 1, cols]
                acc = acc + jnp.where(keep[j], term, F32(0.0))
            h16 = (centre + acc).astype(BF16)
            hid[pl.ds(r0, step), cols] = h16
            h = h16.astype(F32)
            hs.append(h)
            total = total + h
        mean = jnp.sum(total, axis=1, keepdims=True) * F32(1.0 / D)
        hs = [h - mean for h in hs]
        square = jnp.zeros((step, 128), F32)
        for h in hs:
            square = square + h * h
        var = jnp.sum(square, axis=1, keepdims=True) * F32(1.0 / D)
        scale = lax.rsqrt(var + F32(1e-5))
        for c in range(tiles):
            cols = slice(128 * c, 128 * c + 128)
            nrm[pl.ds(d0, step), cols] = (hs[c] * scale * gain[:, cols]).astype(BF16)
        return 0

    lax.fori_loop(first, last, block, 0)


def project(nrm, rows, weights, base, out, pieces):
    value = jnp.dot(
        nrm[rows, :], weights[:, base : base + D], preferred_element_type=F32
    ).astype(BF16)
    at = 0
    for place, size in pieces:
        out[place : place + size, :] = value[at : at + size]
        at += size


def attend(heads, tiles, q, k, v, bias, attn):
    factor = 1.4426950408889634 / 128.0**0.5
    work = []
    for h in heads:
        lanes = pl.ds(pl.multiple_of(h * 128, 128), 128)
        for i in tiles:
            own = slice(128 * i, 128 * i + 128)
            seen = slice(128 * i, 128 * i + 256)
            s = lax.dot_general(
                q[own, lanes], k[seen, lanes], (((1,), (1,)), ((), ())), preferred_element_type=F32
            )
            work.append((own, seen, lanes, s + bias[i]))
    tops = [jnp.max(s, axis=1, keepdims=True) for _, _, _, s in work]
    expos = [jnp.exp2((item[3] - top) * factor) for item, top in zip(work, tops)]
    norms = [1.0 / jnp.sum(e, axis=1, keepdims=True) for e in expos]
    for (own, seen, lanes, _), e, norm in zip(work, expos, norms):
        w = (e * norm).astype(BF16)
        attn[own, lanes] = jnp.dot(w, v[seen, lanes], preferred_element_type=F32).astype(BF16)


def placement_of(row):
    rows = row.shape[1]
    square = lax.broadcasted_iota(jnp.int32, (rows, rows), 0) == lax.broadcasted_iota(
        jnp.int32, (rows, rows), 1
    )
    spread = jnp.where(square, row.astype(F32), F32(0.0))
    owner = jnp.sum(spread, axis=1, keepdims=True).astype(jnp.int32)
    lane = lax.broadcasted_iota(jnp.int32, (rows, 128), 1)
    hot = jnp.where(owner == lane, F32(1.0), F32(0.0))
    lower = jnp.where(
        lax.broadcasted_iota(jnp.int32, (rows, rows), 1)
        < lax.broadcasted_iota(jnp.int32, (rows, rows), 0),
        F32(1.0),
        F32(0.0),
    ).astype(BF16)
    before = jnp.dot(lower, hot.astype(BF16), preferred_element_type=F32)
    rank = jnp.sum(hot * before, axis=1, keepdims=True).astype(jnp.int32)
    slot = owner * 4 + rank
    slot_row = jnp.sum(jnp.where(square, slot.astype(F32), F32(0.0)), axis=0, keepdims=True)
    column = lax.broadcasted_iota(jnp.int32, (128, rows), 0)
    by_slot = jnp.where(column == slot_row.astype(jnp.int32), F32(1.0), F32(0.0)).astype(BF16)
    by_row = jnp.where(lane == slot, F32(1.0), F32(0.0)).astype(BF16)
    return by_slot, by_row


def remote(src, dst, sends, recvs, index, target):
    return pltpu.make_async_remote_copy(
        src_ref=src,
        dst_ref=dst,
        send_sem=sends.at[index],
        recv_sem=recvs.at[index],
        device_id=target,
        device_id_type=MESH,
    )


def each(count, body):
    def one(k, _):
        body(k)
        return 0

    lax.fori_loop(1, count, one, 0)


def to_slots(value, wide, slots):
    for c in range(D // 128):
        wide[pl.ds(c, 128, stride=8), :] = value[:, 128 * c : 128 * c + 128].astype(F32)
    for o in range(N_SEQ):
        slots[o] = wide[32 * o : 32 * o + 32, :].astype(BF16)


def from_slots(slots, wide):
    for o in range(N_SEQ):
        wide[32 * o : 32 * o + 32, :] = slots[o].astype(F32)
    return [wide[pl.ds(c, 128, stride=8), :].astype(BF16) for c in range(D // 128)]


def whole_kernel(
    frames, begins, owner_hbm, taps_hbm, gain_hbm, wqkv_hbm, wout_hbm, cot_hbm,
    audio, fin,
    xb, xf, bgs, dprev, dnext, hid, nrm, edge, qs, ks, vs, bias, attn, wqkv, wout,
    cotv, cots, back, gall, wide, place, pick, ahl, asp, aall, part, tiles, got, aout, arecv,
    owner, taps, gain,
    local_sems, halo_s, halo_r, cot_s, cot_r, g_s, g_r, relay_s, relay_r, a_s, a_r, xz_s, xz_r,
    t_s, t_r, m_s, m_r, h0_s, h0_r, h1_s, h1_r, p0_s, p0_r, p1_s, p1_r, c_s, c_r,
):
    z = lax.axis_index("grp")
    s = lax.axis_index("seq")
    x = s // GROUP
    j = s % GROUP
    y = j // 2
    c = j % 2

    def seq(k):
        return {"seq": (s + k) % N_SEQ}

    def grp(k):
        return {"grp": (z + k) % N_GRP}

    def in_group(k):
        return {"seq": x * GROUP + (j + k) % GROUP}

    def along_x(k):
        return {"seq": (x + k) % N_X * GROUP + j}

    def along_y(k):
        return {"seq": x * GROUP + (y + k) % N_Y * 2 + c}

    other_core = {"seq": x * GROUP + y * 2 + (1 - c)}

    barrier = pltpu.get_barrier_semaphore()

    def greet(target):
        pl.semaphore_signal(barrier, inc=1, device_id=target, device_id_type=MESH)

    def across(k):
        return {"grp": (z + k % N_GRP) % N_GRP, "seq": (x + k // N_GRP) % N_X * GROUP + j}

    each(N_SEQ, lambda k: greet(seq(k)))

    def greet_planes(kz):
        for kx in range(N_X):
            greet(across(kx * N_GRP + kz))

    each(N_GRP, greet_planes)

    def rows_of(source):
        return pl.ds(pl.multiple_of(source * 64, 64), 64)

    loads = [
        pltpu.make_async_copy(begins, bgs.at[3], local_sems.at[0]),
        pltpu.make_async_copy(frames.at[0], xb.at[pl.ds(LEFT, F)], local_sems.at[1]),
        pltpu.make_async_copy(taps_hbm, taps, local_sems.at[2]),
        pltpu.make_async_copy(gain_hbm, gain, local_sems.at[3]),
        pltpu.make_async_copy(cot_hbm.at[0], cotv, local_sems.at[4]),
        pltpu.make_async_copy(owner_hbm, owner, local_sems.at[5]),
        pltpu.make_async_copy(wqkv_hbm, wqkv, local_sems.at[6]),
        pltpu.make_async_copy(wout_hbm, wout, local_sems.at[7]),
    ]
    for copy in loads:
        copy.start()
    for copy in loads[:4]:
        copy.wait()
    none = jnp.zeros((1, F), jnp.int32)
    alone = jnp.concatenate([none, none, none, bgs[3], none[:, :128]], axis=1)
    bounds(alone, s * F, F * N_SEQ, dprev, dnext)
    for tile in range(D // 128):
        xf[tile, LEFT : LEFT + F] = xb[LEFT : LEFT + F, 128 * tile : 128 * tile + 128].astype(F32)
    loads[4].wait()
    to_slots(cotv[...], wide, cots)
    inner = lambda n: (128 + 64 * n, 64 * n)
    conv_norm(xf, taps, gain, dprev, dnext, hid, nrm, 0, 2, inner)
    pl.semaphore_wait(barrier, N_SEQ - 1 + N_X * (N_GRP - 1))

    halo = [
        remote(frames.at[0, pl.ds(F - LEFT, LEFT)], xb.at[pl.ds(0, LEFT)], halo_s, halo_r, 0, seq(1)),
        remote(frames.at[0, pl.ds(0, RIGHT)], xb.at[pl.ds(LEFT + F, RIGHT)], halo_s, halo_r, 1, seq(N_SEQ - 1)),
        remote(begins, bgs.at[2], halo_s, halo_r, 2, seq(1)),
        remote(begins, bgs.at[1], halo_s, halo_r, 3, seq(2)),
        remote(begins, bgs.at[0], halo_s, halo_r, 4, seq(3)),
        remote(begins, bgs.at[4], halo_s, halo_r, 5, seq(N_SEQ - 1)),
    ]
    for copy in halo[2:]:
        copy.start()

    def copy_cot(k):
        return remote(cots.at[(s + k) % N_SEQ], back.at[s], cot_s, cot_r, k, seq(k))

    each(N_SEQ, lambda k: copy_cot(k).start())
    for copy in halo[:2]:
        copy.start()
    back[s] = cots[s]

    conv_norm(xf, taps, gain, dprev, dnext, hid, nrm, 2, 7, inner)
    loads[5].wait()
    place[...], pick[...] = placement_of(owner[...])
    loads[6].wait()
    project(nrm, slice(0, 448), wqkv, 0, qs, ((32, 448),))

    project(nrm, slice(0, 448), wqkv, D, ks, ((128, 448),))
    project(nrm, slice(0, 448), wqkv, 2 * D, vs, ((128, 448),))
    for copy in halo[2:]:
        copy.wait_recv()
    marks = jnp.concatenate([bgs[0], bgs[1], bgs[2], bgs[3], bgs[4][:, :128]], axis=1)
    bounds(marks, s * F, F * N_SEQ, dprev, dnext)
    attention_bias(dprev, dnext, bias)

    def middle(n, _):
        attend([4 * n + h for h in range(4)], (1, 2), qs, ks, vs, bias, attn)
        return 0

    lax.fori_loop(0, 1, middle, 0)

    def got_cot(k):
        source = (s + N_SEQ - k) % N_SEQ
        remote(back.at[source], back.at[source], cot_s, cot_r, k, seq(k)).wait_recv()

    each(N_SEQ, got_cot)
    for tile, value in enumerate(from_slots(back, wide)):
        gall[rows_of(j), 128 * tile : 128 * tile + 128] = jnp.dot(
            pick[...], value, preferred_element_type=F32
        ).astype(BF16)

    def copy_g(k):
        block = gall.at[rows_of(j)]
        return remote(block, block, g_s, g_r, k, along_y(k))

    def copy_relay(k):
        block = gall.at[rows_of((y + N_Y - k) % N_Y * 2 + c)]
        return remote(block, block, relay_s, relay_r, k, other_core)

    for k in (1, 3, 2):
        copy_g(k).start()
    copy_relay(0).start()

    lax.fori_loop(1, HEADS // 4, middle, 0)
    for copy in halo[:2]:
        copy.wait_recv()
    for tile in range(D // 128):
        cols = slice(128 * tile, 128 * tile + 128)
        xf[tile, :LEFT] = xb[:LEFT, cols].astype(F32)
        xf[tile, LEFT + F :] = xb[LEFT + F :, cols].astype(F32)
    conv_norm(
        xf, taps, gain, dprev, dnext, hid, edge, 0, 3,
        lambda n: (64 * n + 448 * (n // 2), 64 * n),
    )
    project(edge, slice(96, 160), wqkv, 0, qs, ((0, 32), (480, 32)))
    project(edge, slice(0, 192), wqkv, D, ks, ((0, 128), (576, 64)))
    project(edge, slice(0, 192), wqkv, 2 * D, vs, ((0, 128), (576, 64)))

    rows = F // SUB
    gather = jnp.where(
        lax.broadcasted_iota(jnp.int32, (rows, F), 1) >> 3
        == lax.broadcasted_iota(jnp.int32, (rows, F), 0),
        F32(1.0),
        F32(0.0),
    ).astype(BF16)

    def copy_a(n):
        return remote(asp.at[(j + n) % HEADS], aall.at[rows_of(j)], a_s, a_r, n, in_group(n))

    def some_heads(*turns):
        pair = [(j + n) % HEADS for n in turns]
        attend(pair, (0, 3), qs, ks, vs, bias, attn)
        for h in pair:
            lanes = pl.ds(pl.multiple_of(h * 128, 128), 128)
            asum = jnp.dot(gather, attn[:, lanes], preferred_element_type=F32)
            high = asum.astype(BF16)
            low = (asum - high.astype(F32)).astype(BF16)
            ahl[:rows, lanes] = high
            ahl[rows:, lanes] = low
            asp[h, :, :128] = high
            asp[h, :, 128:] = low

    some_heads(1, 2, 3, 4)
    for n in (1, 2, 3, 4):
        copy_a(n).start()
    some_heads(5, 6, 7)
    for n in (5, 6, 7):
        copy_a(n).start()
    some_heads(0)
    aall[rows_of(j), :] = asp[j]
    for k in (1, 3, 2):
        copy_g(k).wait_recv()
        copy_relay(k).start()

    dims = (((0,), (0,)), ((), ()))
    for k in range(N_Y):
        copy_relay(k).wait_recv()

    each(GROUP, lambda k: copy_a(k).wait_recv())
    both = lax.dot_general(aall[...], gall[...], dims, preferred_element_type=F32)
    part[...] = both[:128] + both[128:]
    for px in range(N_X):
        for pz in range(N_GRP):
            tiles[px, pz] = part[32 * px : 32 * px + 32, 128 * pz : 128 * pz + 128].astype(BF16)

    def copy_xz(k):
        block = tiles.at[(x + k // N_GRP) % N_X, (z + k % N_GRP) % N_GRP]
        return remote(block, got.at[k], xz_s, xz_r, k, across(k))

    far_first = (4, 3, 5, 2, 6, 1, 7)
    for kz in far_first:
        for kx in range(N_X):
            copy_xz(kx * N_GRP + kz).start()
    for kx in range(1, N_X):
        copy_xz(kx * N_GRP).start()
    loads[7].wait()
    hsum = jnp.dot(gather, hid[KOFF : KOFF + F, :], preferred_element_type=F32)
    proj = jnp.dot(ahl[...], wout[...], preferred_element_type=F32)
    proj = proj[:rows] + proj[rows:]
    pooled = ((hsum + proj) * F32(1.0 / SUB)).astype(BF16)
    outgoing = jnp.dot(place[...], pooled, preferred_element_type=F32)
    to_slots(outgoing, wide, aout)

    def copy_audio(k):
        return remote(aout.at[(s + k) % N_SEQ], arecv.at[s], m_s, m_r, k, seq(k))

    each(N_SEQ, lambda k: copy_audio(k).start())
    arecv[s] = aout[s]
    tile_sum = part[
        pl.ds(pl.multiple_of(x * 32, 32), 32), pl.ds(pl.multiple_of(z * 128, 128), 128)
    ]
    each(N_X * N_GRP, lambda k: copy_xz(k).wait_recv())
    for k in range(1, N_X * N_GRP):
        tile_sum = tile_sum + got[k].astype(F32)
    own_cols = pl.ds(pl.multiple_of(z * 128, 128), 128)
    fin[y, c, x, :, own_cols] = (tile_sum * F32(1.0 / (128 * SUB))).astype(BF16)

    def copy_t(k):
        tile = fin.at[y, c, x, :, own_cols]
        return remote(tile, tile, t_s, t_r, k, grp(k))

    for k in far_first:
        copy_t(k).start()
    for k in range(1, N_GRP):
        copy_t(k).wait_recv()

    first, second = pl.ds(0, D // 2), pl.ds(D // 2, D // 2)

    def copy_h0(k):
        block = fin.at[y, c, x, :, first]
        return remote(block, block, h0_s, h0_r, k, along_x(k))

    def copy_h1(k):
        block = fin.at[y, c, x, :, second]
        return remote(block, block, h1_s, h1_r, k, along_y(k))

    def copy_p0(kx, ky):
        block = fin.at[y, c, (x + N_X - kx) % N_X, :, first]
        return remote(block, block, p0_s, p0_r, kx * N_Y + ky, along_y(ky))

    def copy_p1(ky, kx):
        block = fin.at[(y + N_Y - ky) % N_Y, c, x, :, second]
        return remote(block, block, p1_s, p1_r, ky * N_X + kx, along_x(kx))

    def copy_c(half, ky, kx):
        cols = (first, second)[half]
        block = fin.at[(y + N_Y - ky) % N_Y, c, (x + N_X - kx) % N_X, :, cols]
        return remote(block, block, c_s, c_r, (half * N_Y + ky) * N_X + kx, other_core)

    for k in (1, 3, 2):
        copy_h0(k).start()
        copy_h1(k).start()
    for k in (1, 3, 2):
        copy_p0(0, k).start()
        copy_p1(0, k).start()
    copy_c(0, 0, 0).start()
    copy_c(1, 0, 0).start()
    for k in (1, 3, 2):
        copy_h0(k).wait_recv()
        for ky in (1, 3, 2):
            copy_p0(k, ky).start()
        copy_c(0, 0, k).start()
        copy_h1(k).wait_recv()
        for kx in (1, 3, 2):
            copy_p1(k, kx).start()
        copy_c(1, k, 0).start()

    def got_audio(k):
        source = (s + N_SEQ - k) % N_SEQ
        remote(arecv.at[source], arecv.at[source], m_s, m_r, k, seq(k)).wait_recv()

    each(N_SEQ, got_audio)
    for tile, value in enumerate(from_slots(arecv, wide)):
        audio[:, 128 * tile : 128 * tile + 128] = value

    for other in (0, 1, 3, 2):
        for k in (1, 3, 2):
            copy_p0(other, k).wait_recv()
            copy_c(0, k, other).start()
            copy_p1(other, k).wait_recv()
            copy_c(1, other, k).start()
    for ky in range(N_Y):
        for kx in range(N_X):
            copy_c(0, ky, kx).wait_recv()
            copy_c(1, ky, kx).wait_recv()
    for copy in halo:
        copy.wait_send()

    each(N_SEQ, lambda k: copy_audio(k).wait_send())

    each(N_SEQ, lambda k: copy_cot(k).wait_send())
    each(GROUP, lambda k: copy_a(k).wait_send())
    each(N_X * N_GRP, lambda k: copy_xz(k).wait_send())
    each(N_GRP, lambda k: copy_t(k).wait_send())
    for k in range(1, N_X):
        copy_g(k).wait_send()
        copy_h0(k).wait_send()
        copy_h1(k).wait_send()
    for k in range(N_Y):
        copy_relay(k).wait_send()
        for kx in range(N_X):
            copy_c(0, k, kx).wait_send()
            copy_c(1, k, kx).wait_send()
        for other in range(1, N_X):
            copy_p0(k, other).wait_send()
            copy_p1(k, other).wait_send()


def shards(frames, begins, owner, conv_kernel, norm_gain, w_qkv, w_out, cotangent):
    vm = pl.BlockSpec(memory_space=pltpu.VMEM)
    hbm = pl.BlockSpec(memory_space=pltpu.HBM)
    dma = pltpu.SemaphoreType.DMA
    audio, grad = pl.pallas_call(
        whole_kernel,
        out_shape=(
            jax.ShapeDtypeStruct((128, D), BF16),
            jax.ShapeDtypeStruct((N_Y, 2, N_X, 32, D), BF16),
        ),
        in_specs=[hbm] * 8,
        out_specs=(vm, vm),
        scratch_shapes=[
            pltpu.VMEM((LEFT + F + RIGHT, D), BF16),
            pltpu.VMEM((8, LEFT + F + RIGHT, 128), F32),
            pltpu.VMEM((5, 1, F), jnp.int32),
            pltpu.VMEM((KV, 128), F32),
            pltpu.VMEM((KV, 128), F32),
            pltpu.VMEM((KV, D), BF16),
            pltpu.VMEM((448, D), BF16),
            pltpu.VMEM((192, D), BF16),
            pltpu.VMEM((F, D), BF16),
            pltpu.VMEM((KV, D), BF16),
            pltpu.VMEM((KV, D), BF16),
            pltpu.VMEM((4, 128, 256), F32),
            pltpu.VMEM((F, D), BF16),
            pltpu.VMEM((D, 3 * D), BF16),
            pltpu.VMEM((D, D), BF16),
            pltpu.VMEM((128, D), BF16),
            pltpu.VMEM((N_SEQ, 32, 128), BF16),
            pltpu.VMEM((N_SEQ, 32, 128), BF16),
            pltpu.VMEM((GROUP * 64, D), BF16),
            pltpu.VMEM((1024, 128), F32),
            pltpu.VMEM((128, 64), BF16),
            pltpu.VMEM((64, 128), BF16),
            pltpu.VMEM((128, D), BF16),
            pltpu.VMEM((HEADS, 64, 256), BF16),
            pltpu.VMEM((GROUP * 64, 256), BF16),
            pltpu.VMEM((128, D), F32),
            pltpu.VMEM((N_X, N_GRP, 32, 128), BF16),
            pltpu.VMEM((N_X * N_GRP, 32, 128), BF16),
            pltpu.VMEM((N_SEQ, 32, 128), BF16),
            pltpu.VMEM((N_SEQ, 32, 128), BF16),
            pltpu.VMEM((1, 64), jnp.int32),
            pltpu.VMEM((9, D), F32),
            pltpu.VMEM((1, D), F32),
            dma((8,)),
            dma((6,)), dma((6,)),
            dma((N_SEQ,)), dma((N_SEQ,)),
            dma((N_Y,)), dma((N_Y,)),
            dma((N_Y,)), dma((N_Y,)),
            dma((GROUP,)), dma((GROUP,)),
            dma((N_X * N_GRP,)), dma((N_X * N_GRP,)),
            dma((N_GRP,)), dma((N_GRP,)),
            dma((N_SEQ,)), dma((N_SEQ,)),
            dma((N_X,)), dma((N_X,)),
            dma((N_Y,)), dma((N_Y,)),
            dma((N_X * N_Y,)), dma((N_X * N_Y,)),
            dma((N_X * N_Y,)), dma((N_X * N_Y,)),
            dma((2 * N_Y * N_X,)), dma((2 * N_Y * N_X,)),
        ],
        compiler_params=pltpu.CompilerParams(
            vmem_limit_bytes=48 * 1024 * 1024, collective_id=0, has_side_effects=True
        ),
        name="whole",
    )(
        *(
            pltpu.with_memory_space_constraint(value, pltpu.HBM)
            for value in (
                frames,
                begins,
                owner.reshape(1, 64),
                conv_kernel,
                norm_gain.reshape(1, D),
                w_qkv,
                w_out,
                cotangent,
            )
        )
    )
    return audio.reshape(1, 128, D), grad.reshape(D, D)


def solution(mesh):
    return jax.shard_map(
        shards,
        mesh=mesh,
        in_specs=(
            P("grp", "seq", None),
            P("grp", "seq"),
            P("grp", "seq", None),
            P(),
            P(),
            P(),
            P(),
            P("grp", "seq", None),
        ),
        out_specs=(P("grp", "seq", None), P()),
        check_vma=False,
    )
```
